32 devices in a mesh: gx: 16 (over z, y, core), gy: 2 (over x).
Axes of the slice: x: 2, y: 2, z: 4, core: 2. Of those that a mesh axis runs over, the one named last changes fastest.
Arguments:
- e_field: float32 [3, 64, 128, 256], P(None, None, 'gx', 'gy'), may hold values from -6 to 6
- h_field: float32 [3, 64, 128, 256], P(None, None, 'gx', 'gy'), may hold values from -6 to 6
- material: int32 [64, 128, 256], P(None, 'gx', 'gy'), may hold values from 0 to 7
- permittivity: float32 [8], replicated, may hold values from 1 to 12
- conductivity: float32 [8], replicated, may hold values from 0.05 to 2
- src_shift: int32 [256, 2], P(('gx', 'gy')), may hold values from 0 to 128
- src_weight: float32 [256], P(('gx', 'gy')), may hold values from 0.05 to 5
- pupil_mask: int32 [128, 128], replicated, may hold values 0 or 1
Outputs:
- image: float32 [512, 512], P(('gx', 'gy'))
- e_final: float32 [3, 64, 128, 256], P(None, None, 'gx', 'gy')
- h_final: float32 [3, 64, 128, 256], P(None, None, 'gx', 'gy')
The draws below stay inside these ranges and needn't reach their ends.
All inputs are finite; a program needn't handle non-finite values.
Results may differ from the reference program's by a relative error of at most 0.0019.
Values may be sent and summed in bfloat16 or wider, within the bound.
A program may use at most 128 MiB of HBM per device.

```python
import math
import jax
import jax.numpy as jnp
from jax import lax

NZ = 64
STEPS = 4
MATS = 8
K = 256
PW = 128
IMG = 512
NX = 128
NY = 256
SOURCES = 256


def with_ends(drawn, rng, low, largest):
    longest = drawn.shape.index(max(drawn.shape))
    spots = []
    for shift in (0, 1):
        where = [jax.random.randint(jax.random.fold_in(rng, axis), (), 0, length) for axis, length in enumerate(drawn.shape)]
        where[longest] = (where[longest] + shift) % drawn.shape[longest]
        spots.append(tuple(where))
    return drawn.at[spots[0]].set(low).at[spots[1]].set(largest)


def steps_of(stream_key, extent, split, least, largest):
    loudness, own = 1.0, jax.random.fold_in(stream_key, 6)
    for position, blocks in split:
        draws = jnp.exp(jax.random.uniform(jax.random.fold_in(own, position), (blocks,), jnp.float32, least / len(split), largest / len(split)))
        loudness = loudness * jnp.repeat(draws, extent[position] // blocks).reshape([-1 if axis == position else 1 for axis in range(len(extent))])
    return loudness


def scatter_about(own_key, dims, width, limit, shards=(), kind=jnp.bfloat16):
    result = width * jax.random.normal(own_key, dims, jnp.float32)
    if shards:
        result = result * steps_of(own_key, dims, shards, -0.22, 0.18)
    return jnp.clip(result, -limit, limit).astype(kind)


def setup_inputs(seed: int = 0) -> dict:
    splits = jax.random.split(jax.random.key(seed), 9)
    e_field = scatter_about(splits[0], (3, NZ, NX, NY), 1.0, 6.0, ((2, 16), (3, 2)), jnp.float32)
    h_field = scatter_about(splits[1], (3, NZ, NX, NY), 1.0, 6.0, ((2, 16), (3, 2)), jnp.float32)
    material = with_ends(jax.random.randint(splits[2], (NZ, NX, NY), 0, MATS), jax.random.fold_in(splits[2], 1), 0, MATS - 1).astype(jnp.int32)
    permittivity = jnp.clip(jnp.exp(jax.random.uniform(splits[3], (MATS,), jnp.float32, math.log(1.0), math.log(12.0))), 1.0, 12.0)
    conductivity = jnp.clip(jnp.exp(jax.random.uniform(splits[4], (MATS,), jnp.float32, math.log(0.05), math.log(2.0))), 0.05, 2.0)
    src_shift = with_ends(jax.random.randint(splits[5], (SOURCES, 2), 0, K - PW + 1), jax.random.fold_in(splits[5], 1), 0, K - PW).astype(jnp.int32)
    src_weight = jnp.clip(jnp.exp(math.log(5.0) - 4.6051702 * jax.random.uniform(splits[6], (SOURCES,), jnp.float32) ** steps_of(splits[6], (SOURCES,), ((0, 32),), -0.2, 0.2)), 0.05, 5.0)
    pupil_mask = with_ends((jax.random.randint(splits[7], (PW, PW), 0, 4) < 3).astype(jnp.int32), jax.random.fold_in(splits[7], 1), 0, 1)
    return dict(e_field=e_field, h_field=h_field, material=material, permittivity=permittivity, conductivity=conductivity, src_shift=src_shift, src_weight=src_weight, pupil_mask=pupil_mask)


COURANT = 0.5

def coefficients(material, permittivity, conductivity):
    loss = conductivity / (2.0 * permittivity)
    keep_tab = (1.0 - loss) / (1.0 + loss)
    drive_tab = COURANT / (permittivity * (1.0 + loss))
    keep = jnp.zeros(material.shape, jnp.float32)
    drive = jnp.zeros(material.shape, jnp.float32)
    for index in range(permittivity.shape[0]):
        chosen = material == index
        keep = jnp.where(chosen, keep_tab[index], keep)
        drive = jnp.where(chosen, drive_tab[index], drive)
    return (keep, drive)

def zero_face(field, axis):
    shape = list(field.shape)
    shape[axis] = 1
    return jnp.zeros(shape, field.dtype)

def ahead(field, face, axis):
    count = field.shape[axis]
    return jnp.concatenate((lax.slice_in_dim(field, 1, count, axis=axis), face), axis=axis)

def behind(field, face, axis):
    count = field.shape[axis]
    return jnp.concatenate((face, lax.slice_in_dim(field, 0, count - 1, axis=axis)), axis=axis)

def magnetic(e, h, faces_x, faces_y):
    ex, ey, ez = (e[0], e[1], e[2])
    ey_x = ahead(ey, faces_x[0], 1)
    ez_x = ahead(ez, faces_x[1], 1)
    ex_y = ahead(ex, faces_y[0], 2)
    ez_y = ahead(ez, faces_y[1], 2)
    ex_z = ahead(ex, zero_face(ex, 0), 0)
    ey_z = ahead(ey, zero_face(ey, 0), 0)
    new_x = h[0] - COURANT * (ez_y - ez - (ey_z - ey))
    new_y = h[1] - COURANT * (ex_z - ex - (ez_x - ez))
    new_z = h[2] - COURANT * (ey_x - ey - (ex_y - ex))
    return jnp.stack((new_x, new_y, new_z))

def electric(e, h, keep, drive, faces_x, faces_y):
    hx, hy, hz = (h[0], h[1], h[2])
    hy_x = behind(hy, faces_x[0], 1)
    hz_x = behind(hz, faces_x[1], 1)
    hx_y = behind(hx, faces_y[0], 2)
    hz_y = behind(hz, faces_y[1], 2)
    hx_z = behind(hx, zero_face(hx, 0), 0)
    hy_z = behind(hy, zero_face(hy, 0), 0)
    new_x = keep * e[0] + drive * (hz - hz_y - (hy - hy_z))
    new_y = keep * e[1] + drive * (hx - hx_z - (hz - hz_x))
    new_z = keep * e[2] + drive * (hy - hy_x - (hx - hx_y))
    return jnp.stack((new_x, new_y, new_z))

def exit_spectrum(near, row_start, col_start, rows_all, cols_all, order):
    count_x = near.shape[1]
    count_y = near.shape[2]
    freqs = jnp.arange(order, dtype=jnp.int32) - order // 2
    cols = col_start + jnp.arange(count_y, dtype=jnp.int32)
    phase_y = jnp.mod(cols[:, None] * freqs[None, :], cols_all).astype(jnp.float32) * (2.0 * math.pi / cols_all)
    table_y = jnp.concatenate((jnp.cos(phase_y), -jnp.sin(phase_y)), axis=1)
    half = jnp.dot(near.reshape(2 * count_x, count_y), table_y, precision=lax.Precision.HIGHEST)
    half = half.reshape(2, count_x, 2 * order)
    rows = row_start + jnp.arange(count_x, dtype=jnp.int32)
    phase_x = jnp.mod(freqs[:, None] * rows[None, :], rows_all).astype(jnp.float32) * (2.0 * math.pi / rows_all)
    table_x = jnp.concatenate((jnp.cos(phase_x), jnp.sin(phase_x)), axis=0)
    blocks = jnp.einsum('ax,pxb->pab', table_x, half, precision=lax.Precision.HIGHEST)
    real = blocks[:, :order, :order] + blocks[:, order:, order:]
    imag = blocks[:, :order, order:] - blocks[:, order:, :order]
    stacked = jnp.stack((real[0], imag[0], real[1], imag[1]), axis=1)
    return stacked * (1.0 / math.sqrt(rows_all * cols_all))

def pupil_tables(window, pixels):
    offsets = jnp.arange(window, dtype=jnp.int32) - window // 2
    places = jnp.arange(pixels, dtype=jnp.int32)
    phase = jnp.mod(offsets[:, None] * places[None, :], pixels).astype(jnp.float32) * (2.0 * math.pi / pixels)
    cosine = jnp.cos(phase)
    sine = jnp.sin(phase)
    second = jnp.concatenate((jnp.concatenate((cosine, sine), axis=1), jnp.concatenate((-sine, cosine), axis=1)), axis=0)
    row_cos = cosine.T / window
    row_sin = sine.T / window
    real_row = jnp.stack((row_cos, -row_sin), axis=2)
    imag_row = jnp.stack((row_sin, row_cos), axis=2)
    first = jnp.stack((real_row, imag_row)).reshape(2, pixels, 2 * window)
    return (second.astype(jnp.bfloat16), first.astype(jnp.bfloat16))

def pupil_halves(spectrum_b, shifts, pupil_mask, second, window, pixels):
    zero = jnp.zeros((), jnp.int32)

    def cut(shift):
        return lax.dynamic_slice(spectrum_b, (shift[0].astype(jnp.int32), zero, shift[1].astype(jnp.int32)), (window, 4, window))
    pieces = jax.vmap(cut)(shifts)
    pieces = pieces * pupil_mask.astype(jnp.bfloat16)[None, :, None, :]
    count = shifts.shape[0]
    arranged = pieces.reshape(count, window, 2, 2, window).transpose(0, 2, 1, 3, 4).reshape(count * 2 * window, 2 * window)
    halves = jnp.dot(arranged, second, preferred_element_type=jnp.float32).astype(jnp.bfloat16)
    return halves.reshape(count * 2, 2 * window, pixels)

def reference(e_field, h_field, material, permittivity, conductivity, src_shift, src_weight, pupil_mask):
    keep, drive = coefficients(material, permittivity, conductivity)
    e = e_field
    h = h_field
    for step in range(STEPS):
        faces_x = (zero_face(e[1], 1), zero_face(e[2], 1))
        faces_y = (zero_face(e[0], 2), zero_face(e[2], 2))
        h = magnetic(e, h, faces_x, faces_y)
        faces_x = (zero_face(h[1], 1), zero_face(h[2], 1))
        faces_y = (zero_face(h[0], 2), zero_face(h[2], 2))
        e = electric(e, h, keep, drive, faces_x, faces_y)
    near = e[0:2, NZ - 1]
    spectrum = exit_spectrum(near, 0, 0, NX, NY, K)
    spectrum_b = spectrum.astype(jnp.bfloat16)
    second, first = pupil_tables(PW, IMG)
    flat_first = first.reshape(2 * IMG, 2 * PW)
    total_sources = src_shift.shape[0]

    def add(image, item):
        shift, weight = item
        halves = pupil_halves(spectrum_b, shift[None, :], pupil_mask, second, PW, IMG)
        for pol in range(2):
            field = jnp.dot(flat_first, halves[pol], preferred_element_type=jnp.float32)
            image = image + weight / total_sources * (field[:IMG] * field[:IMG] + field[IMG:] * field[IMG:])
        return (image, None)
    image, _ = lax.scan(add, jnp.zeros((IMG, IMG), jnp.float32), (src_shift, src_weight))
    return (image, e, h)
```

```python
import math

import jax
import jax.numpy as jnp
import numpy as np
from jax import lax
from jax.sharding import PartitionSpec as P

STEPS = 4
K = 256
PW = 128
IMG = 512


COURANT = 0.5


def passed_along(value, axis, steps):
    count = lax.axis_size(axis)
    first, last = (max(0, -steps), min(count, count - steps))
    return lax.ppermute(value, axis, [(source, source + steps) for source in range(first, last)])


def coefficients(material, permittivity, conductivity):
    loss = conductivity / (2.0 * permittivity)
    keep_tab = (1.0 - loss) / (1.0 + loss)
    drive_tab = COURANT / (permittivity * (1.0 + loss))
    keep = jnp.zeros(material.shape, jnp.float32)
    drive = jnp.zeros(material.shape, jnp.float32)
    for index in range(permittivity.shape[0]):
        chosen = material == index
        keep = jnp.where(chosen, keep_tab[index], keep)
        drive = jnp.where(chosen, drive_tab[index], drive)
    return (keep, drive)


def zero_face(field, axis):
    shape = list(field.shape)
    shape[axis] = 1
    return jnp.zeros(shape, field.dtype)


def ahead(field, face, axis):
    count = field.shape[axis]
    return jnp.concatenate((lax.slice_in_dim(field, 1, count, axis=axis), face), axis=axis)


def behind(field, face, axis):
    count = field.shape[axis]
    return jnp.concatenate((face, lax.slice_in_dim(field, 0, count - 1, axis=axis)), axis=axis)


def magnetic(e, h, faces_x, faces_y):
    ex, ey, ez = (e[0], e[1], e[2])
    ey_x = ahead(ey, faces_x[0], 1)
    ez_x = ahead(ez, faces_x[1], 1)
    ex_y = ahead(ex, faces_y[0], 2)
    ez_y = ahead(ez, faces_y[1], 2)
    ex_z = ahead(ex, zero_face(ex, 0), 0)
    ey_z = ahead(ey, zero_face(ey, 0), 0)
    new_x = h[0] - COURANT * (ez_y - ez - (ey_z - ey))
    new_y = h[1] - COURANT * (ex_z - ex - (ez_x - ez))
    new_z = h[2] - COURANT * (ey_x - ey - (ex_y - ex))
    return jnp.stack((new_x, new_y, new_z))


def electric(e, h, keep, drive, faces_x, faces_y):
    hx, hy, hz = (h[0], h[1], h[2])
    hy_x = behind(hy, faces_x[0], 1)
    hz_x = behind(hz, faces_x[1], 1)
    hx_y = behind(hx, faces_y[0], 2)
    hz_y = behind(hz, faces_y[1], 2)
    hx_z = behind(hx, zero_face(hx, 0), 0)
    hy_z = behind(hy, zero_face(hy, 0), 0)
    new_x = keep * e[0] + drive * (hz - hz_y - (hy - hy_z))
    new_y = keep * e[1] + drive * (hx - hx_z - (hz - hz_x))
    new_z = keep * e[2] + drive * (hy - hy_x - (hx - hx_y))
    return jnp.stack((new_x, new_y, new_z))


def spectrum_tables(rows_all, cols_all, order):
    freqs = np.arange(order) - order // 2
    phase_y = 2.0 * np.pi * np.mod(np.arange(cols_all)[:, None] * freqs[None, :], cols_all) / cols_all
    table_y = np.concatenate((np.cos(phase_y), -np.sin(phase_y)), axis=1)
    phase_x = 2.0 * np.pi * np.mod(freqs[:, None] * np.arange(rows_all)[None, :], rows_all) / rows_all
    table_x = np.concatenate((np.cos(phase_x), np.sin(phase_x)), axis=1) / np.sqrt(rows_all * cols_all)
    return table_y.astype(np.float32), table_x.astype(np.float32)


def image_tables(window, pixels):
    coarse = pixels // 2
    offsets = np.arange(window) - window // 2
    phase = 2.0 * np.pi * np.mod(offsets[:, None] * np.arange(coarse)[None, :], coarse) / coarse
    cosine, sine = np.cos(phase), np.sin(phase)
    second = np.block([[cosine, sine], [-sine, cosine]])
    first = np.block([[cosine.T, -sine.T], [sine.T, cosine.T]]) / window
    gaps = np.arange(pixels)[:, None] - 2 * np.arange(coarse)[None, :]
    spread = np.ones(gaps.shape)
    for order in range(1, coarse // 2):
        spread += 2.0 * np.cos(2.0 * np.pi * np.mod(order * gaps, pixels) / pixels)
    spread += np.cos(np.pi * gaps / 2.0)
    spread = spread / coarse
    return second.astype(jnp.bfloat16), first.astype(jnp.bfloat16), spread.astype(np.float32)


def exit_spectrum(near, order):
    rows_all, cols_all = near.shape[1], near.shape[2]
    table_y, table_x = spectrum_tables(rows_all, cols_all, order)
    half = jnp.einsum("pxy,yb->pxb", near, table_y, precision=lax.Precision.HIGHEST)
    real, imag = half[:, :, :order], half[:, :, order:]
    both = jnp.concatenate(
        (jnp.concatenate((real, imag), axis=2), jnp.concatenate((imag, -real), axis=2)), axis=1
    )
    return jnp.einsum("ax,pxb->pab", table_x, both, precision=lax.Precision.HIGHEST)


def local(
    e_field, h_field, material, permittivity, conductivity, src_shift, src_weight, pupil_mask
):
    depth = e_field.shape[1]
    devices = lax.axis_size("gx") * lax.axis_size("gy")
    keep, drive = coefficients(material, permittivity, conductivity)
    e = e_field
    h = h_field
    for step in range(STEPS):
        upper = passed_along(jnp.stack((e[1][:, :1], e[2][:, :1])), "gx", -1)
        right = passed_along(jnp.stack((e[0][:, :, :1], e[2][:, :, :1])), "gy", -1)
        h = magnetic(e, h, (upper[0], upper[1]), (right[0], right[1]))
        lower = passed_along(jnp.stack((h[1][:, -1:], h[2][:, -1:])), "gx", 1)
        left = passed_along(jnp.stack((h[0][:, :, -1:], h[2][:, :, -1:])), "gy", 1)
        e = electric(e, h, keep, drive, (lower[0], lower[1]), (left[0], left[1]))
    near = e[0:2, depth - 1]
    whole = lax.all_gather(near, ("gx", "gy"))
    whole = whole.reshape((lax.axis_size("gx"), lax.axis_size("gy")) + near.shape)
    whole = whole.transpose(2, 0, 3, 1, 4).reshape(
        2, near.shape[1] * lax.axis_size("gx"), near.shape[2] * lax.axis_size("gy")
    )
    spectrum = exit_spectrum(whole, K).astype(jnp.bfloat16)
    second, first, spread = image_tables(PW, IMG)
    zero = jnp.zeros((), jnp.int32)
    parts = spectrum.reshape(2, K, 2, K)

    def cut(shift):
        return lax.dynamic_slice(parts, (zero, shift[0], zero, shift[1]), (2, PW, 2, PW))

    count = src_shift.shape[0]
    pieces = jax.vmap(cut)(src_shift) * pupil_mask.astype(jnp.bfloat16)[None, None, :, None, :]
    arranged = pieces.reshape(count * 2 * PW, 2 * PW)
    halves = jnp.dot(arranged, second, preferred_element_type=jnp.float32).astype(jnp.bfloat16)
    coarse = IMG // 2
    halves = halves.reshape(count * 2, PW, 2, coarse).transpose(0, 2, 1, 3)
    halves = halves.reshape(count * 2, 2 * PW, coarse)
    factors = jnp.repeat(src_weight / (count * devices), 2)

    def add(total, item):
        field = jnp.dot(first, item[0], preferred_element_type=jnp.float32)
        return (
            total + item[1] * (field[:coarse] * field[:coarse] + field[coarse:] * field[coarse:]),
            None,
        )

    total, _ = lax.scan(add, jnp.zeros((coarse, coarse), jnp.float32), (halves, factors), unroll=4)
    tall = jnp.dot(spread, total, precision=lax.Precision.HIGHEST).astype(jnp.bfloat16)
    blocks = lax.all_to_all(
        tall.reshape(devices, IMG // devices, coarse), ("gx", "gy"), 0, 0, tiled=True
    )
    owned = jnp.sum(blocks.astype(jnp.float32), axis=0)
    image = jnp.dot(owned, spread.T, precision=lax.Precision.HIGHEST)
    return (image, e, h)


def solution(mesh):
    return jax.shard_map(
        local,
        mesh=mesh,
        in_specs=(
            P(None, None, "gx", "gy"),
            P(None, None, "gx", "gy"),
            P(None, "gx", "gy"),
            P(),
            P(),
            P(("gx", "gy"), None),
            P(("gx", "gy")),
            P(),
        ),
        out_specs=(P(("gx", "gy"), None), P(None, None, "gx", "gy"), P(None, None, "gx", "gy")),
        check_vma=False,
    )
```

```python
import functools

import jax
import jax.numpy as jnp
import numpy as np
from jax import lax
from jax.experimental import pallas as pl
from jax.experimental.pallas import tpu as pltpu
from jax.sharding import PartitionSpec as P

STEPS = 4
K = 256
PW = 128
IMG = 512
COURANT = 0.5
MESH = pl.DeviceIdType.MESH
HIGHEST = lax.Precision.HIGHEST
VMEM = pl.BlockSpec(memory_space=pltpu.VMEM)
SMEM = pl.BlockSpec(memory_space=pltpu.SMEM)
ANY = pl.BlockSpec(memory_space=pl.ANY)


def spectrum_tables(rows_all, cols_all, order):
    freqs = np.arange(order) - order // 2
    phase_y = 2.0 * np.pi * np.mod(np.arange(cols_all)[:, None] * freqs[None, :], cols_all) / cols_all
    table_y = np.concatenate((np.cos(phase_y), -np.sin(phase_y)), axis=1)
    phase_x = 2.0 * np.pi * np.mod(freqs[:, None] * np.arange(rows_all)[None, :], rows_all) / rows_all
    table_x = np.concatenate((np.cos(phase_x), np.sin(phase_x)), axis=1) / np.sqrt(rows_all * cols_all)
    return table_y.astype(np.float32), table_x.astype(np.float32)


def image_tables(window, pixels):
    coarse = pixels // 2
    offsets = np.arange(window) - window // 2
    phase = 2.0 * np.pi * np.mod(offsets[:, None] * np.arange(coarse)[None, :], coarse) / coarse
    cosine, sine = np.cos(phase), np.sin(phase)
    second = np.block([[cosine, sine], [-sine, cosine]])
    first = np.block([[cosine.T, -sine.T], [sine.T, cosine.T]]) / window
    gaps = np.arange(pixels)[:, None] - 2 * np.arange(coarse)[None, :]
    spread = np.ones(gaps.shape)
    for order in range(1, coarse // 2):
        spread += 2.0 * np.cos(2.0 * np.pi * np.mod(order * gaps, pixels) / pixels)
    spread += np.cos(np.pi * gaps / 2.0)
    spread = spread / coarse
    return second.astype(jnp.bfloat16), first.astype(jnp.bfloat16), spread.astype(np.float32)


def greet_all(nx, ny, me):
    barrier = pltpu.get_barrier_semaphore()

    def greet(step, carry):
        other = lax.rem(me + step, nx * ny)
        pl.semaphore_signal(
            barrier, inc=1, device_id=(other // ny, lax.rem(other, ny)), device_id_type=MESH
        )
        return carry

    lax.fori_loop(1, nx * ny, greet, 0)
    pl.semaphore_wait(barrier, nx * ny - 1)


def fields_kernel(
    nx, ny, perm, cond, e_in, h_in, mat_in, e_out, h_out, near,
    e, h, mat, keep, drive, edge_x, face_x, face_y, got_x, got_y, in_sem, x_send, x_recv, y_send, y_recv,
    n_send, n_recv,
):
    depth = mat.shape[0]
    rows, cols = mat.shape[1], mat.shape[2]
    gx, gy = lax.axis_index("gx"), lax.axis_index("gy")
    me = gx * ny + gy
    loads = (
        pltpu.make_async_copy(e_in, e.at[:, pl.ds(0, depth)], in_sem.at[0]),
        pltpu.make_async_copy(h_in, h.at[:, pl.ds(1, depth)], in_sem.at[1]),
        pltpu.make_async_copy(mat_in, mat, in_sem.at[2]),
    )
    for load in loads:
        load.start()
    got_x[...] = jnp.zeros_like(got_x)
    got_y[...] = jnp.zeros_like(got_y)
    greet_all(nx, ny, me)
    zero = jnp.zeros((rows, cols), jnp.float32)
    for c in range(3):
        e[c, depth] = zero
        h[c, 0] = zero
    lane = lax.broadcasted_iota(jnp.int32, (rows, cols), 1)
    row = lax.broadcasted_iota(jnp.int32, (rows, cols), 0)
    keeps, drives = [], []
    for m in range(perm.shape[0]):
        loss = cond[m] / (2.0 * perm[m])
        keeps.append((1.0 - loss) / (1.0 + loss))
        drives.append(COURANT / (perm[m] * (1.0 + loss)))

    def x_copy(turn):
        to = gx - 1 if turn % 2 == 0 else gx + 1
        return pltpu.make_async_remote_copy(
            src_ref=face_x.at[turn], dst_ref=got_x.at[turn], send_sem=x_send.at[turn],
            recv_sem=x_recv.at[turn], device_id=(to, gy), device_id_type=MESH,
        )

    def y_copy(turn):
        to = gy - 1 if turn % 2 == 0 else gy + 1
        return pltpu.make_async_remote_copy(
            src_ref=face_y.at[turn], dst_ref=got_y.at[turn], send_sem=y_send.at[turn],
            recv_sem=y_recv.at[turn], device_id=(gx, to), device_id_type=MESH,
        )

    def sends(turn):
        if turn % 2 == 0:
            return gx > 0, gy > 0
        return gx < nx - 1, gy < ny - 1

    def gets(turn):
        if turn % 2 == 0:
            return gx < nx - 1, gy < ny - 1
        return gx > 0, gy > 0

    def start(turn):
        field, base, edge, first, second = (e, 0, 0, 0, 2) if turn % 2 == 0 else (h, 1, cols - 1, 0, 2)
        at_row = 0 if turn % 2 == 0 else rows - 1
        x_to, y_to = sends(turn)
        for k, c in enumerate((1, 2)):
            face_x[turn, k] = field[c, pl.ds(base, depth), at_row, :].astype(jnp.bfloat16)

        @pl.when(x_to)
        def _():
            x_copy(turn).start()

        def pack(z, face):
            for k, c in enumerate((first, second)):
                spot = k * depth + z
                moved = pltpu.roll(field[c, base + z], lax.rem(spot - edge + cols, cols), 1)
                face = jnp.where(lane == spot, moved, face)
            return face

        face_y[turn] = lax.fori_loop(0, depth, pack, zero, unroll=8)

        @pl.when(y_to)
        def _():
            y_copy(turn).start()

    def arrive(turn):
        x_from, y_from = gets(turn)

        @pl.when(y_from)
        def _():
            y_copy(turn).wait_recv()

        @pl.when(x_from)
        def _():
            x_copy(turn).wait_recv()

    def magnetic(turn):
        face = got_y[turn]
        edge_x[...] = got_x[turn].astype(jnp.float32)

        def at(z, carry):
            ex, ey, ez = e[0, z], e[1, z], e[2, z]
            ex_z, ey_z = e[0, z + 1], e[1, z + 1]
            last_row, last_lane = row == rows - 1, lane == cols - 1
            ey_f = edge_x[0, pl.ds(z, 1), :]
            ez_f = edge_x[1, pl.ds(z, 1), :]
            ex_f = pltpu.roll(face, cols - 1 - z, 1)
            ez_g = pltpu.roll(face, cols - 1 - depth - z, 1)
            ey_x = jnp.where(last_row, ey_f, pltpu.roll(ey, rows - 1, 0))
            ez_x = jnp.where(last_row, ez_f, pltpu.roll(ez, rows - 1, 0))
            ex_y = jnp.where(last_lane, ex_f, pltpu.roll(ex, cols - 1, 1))
            ez_y = jnp.where(last_lane, ez_g, pltpu.roll(ez, cols - 1, 1))
            h[0, z + 1] = h[0, z + 1] - COURANT * (ez_y - ez - (ey_z - ey))
            h[1, z + 1] = h[1, z + 1] - COURANT * (ex_z - ex - (ez_x - ez))
            h[2, z + 1] = h[2, z + 1] - COURANT * (ey_x - ey - (ex_y - ex))
            return carry

        lax.fori_loop(0, depth, at, 0, unroll=8)

    def electric(turn):
        face = got_y[turn]
        edge_x[...] = got_x[turn].astype(jnp.float32)

        def at(z, carry):
            hx, hy, hz = h[0, z + 1], h[1, z + 1], h[2, z + 1]
            hx_z, hy_z = h[0, z], h[1, z]
            first_row, first_lane = row == 0, lane == 0
            hy_f = edge_x[0, pl.ds(z, 1), :]
            hz_f = edge_x[1, pl.ds(z, 1), :]
            hx_f = pltpu.roll(face, lax.rem(cols - z, cols), 1)
            hz_g = pltpu.roll(face, cols - depth - z, 1)
            hy_x = jnp.where(first_row, hy_f, pltpu.roll(hy, 1, 0))
            hz_x = jnp.where(first_row, hz_f, pltpu.roll(hz, 1, 0))
            hx_y = jnp.where(first_lane, hx_f, pltpu.roll(hx, 1, 1))
            hz_y = jnp.where(first_lane, hz_g, pltpu.roll(hz, 1, 1))
            kept, driven = keep[z], drive[z]
            e[0, z] = kept * e[0, z] + driven * (hz - hz_y - (hy - hy_z))
            e[1, z] = kept * e[1, z] + driven * (hx - hx_z - (hz - hz_x))
            e[2, z] = kept * e[2, z] + driven * (hy - hy_x - (hx - hx_y))
            return carry

        lax.fori_loop(0, depth, at, 0, unroll=8)

    loads[0].wait()
    start(0)
    loads[2].wait()

    def look_up(z, carry):
        index = mat[z]
        kept, driven = zero, zero
        for m in range(len(keeps)):
            chosen = index == m
            kept = jnp.where(chosen, keeps[m], kept)
            driven = jnp.where(chosen, drives[m], driven)
        keep[z] = kept
        drive[z] = driven
        return carry

    lax.fori_loop(0, depth, look_up, 0, unroll=4)
    loads[1].wait()
    for turn in range(2 * STEPS):
        if turn:
            start(turn)
        arrive(turn)
        if turn % 2 == 0:
            magnetic(turn)
        else:
            electric(turn)

    store_h = pltpu.make_async_copy(h.at[:, pl.ds(1, depth)], h_out, in_sem.at[1])
    store_e = pltpu.make_async_copy(e.at[:, pl.ds(0, depth)], e_out, in_sem.at[0])
    store_h.start()
    store_e.start()

    def spot(index):
        x_at = pl.multiple_of((index // ny) * rows, rows)
        y_at = pl.multiple_of(lax.rem(index, ny) * cols, cols)
        return near.at[:, pl.ds(x_at, rows), pl.ds(y_at, cols)]

    def near_copy(step, other, place):
        return pltpu.make_async_remote_copy(
            src_ref=e.at[pl.ds(0, 2), depth - 1], dst_ref=spot(place), send_sem=n_send.at[step],
            recv_sem=n_recv.at[step], device_id=(other // ny, lax.rem(other, ny)), device_id_type=MESH,
        )

    def push(step, carry):
        near_copy(step, lax.rem(me + step, nx * ny), me).start()
        return carry

    lax.fori_loop(1, nx * ny, push, 0)
    own = pltpu.make_async_copy(e.at[pl.ds(0, 2), depth - 1], spot(me), n_send.at[0])
    own.start()
    own.wait()

    def take(step, carry):
        copy = near_copy(
            step, lax.rem(me + step, nx * ny), lax.rem(me - step + nx * ny, nx * ny)
        )
        copy.wait_recv()
        copy.wait_send()
        return carry

    lax.fori_loop(1, nx * ny, take, 0)
    for turn in range(2 * STEPS):
        x_to, y_to = sends(turn)

        @pl.when(x_to)
        def _():
            x_copy(turn).wait_send()

        @pl.when(y_to)
        def _():
            y_copy(turn).wait_send()

    store_h.wait()
    store_e.wait()


def run_fields(e_field, h_field, material, permittivity, conductivity, nx, ny):
    _, depth, rows, cols = e_field.shape
    devices, turns = nx * ny, 2 * STEPS
    f32, dma = jnp.float32, pltpu.SemaphoreType.DMA
    return pl.pallas_call(
        functools.partial(fields_kernel, nx, ny),
        out_shape=(
            jax.ShapeDtypeStruct(e_field.shape, f32),
            jax.ShapeDtypeStruct(h_field.shape, f32),
            jax.ShapeDtypeStruct((2, rows * nx, cols * ny), f32),
        ),
        in_specs=[SMEM, SMEM, ANY, ANY, ANY],
        out_specs=(ANY, ANY, VMEM),
        scratch_shapes=[
            pltpu.VMEM((3, depth + 1, rows, cols), f32),
            pltpu.VMEM((3, depth + 1, rows, cols), f32),
            pltpu.VMEM((depth, rows, cols), jnp.int32),
            pltpu.VMEM((depth, rows, cols), f32),
            pltpu.VMEM((depth, rows, cols), f32),
            pltpu.VMEM((2, depth, cols), f32),
            pltpu.VMEM((turns, 2, depth, cols), jnp.bfloat16),
            pltpu.VMEM((turns, rows, cols), f32),
            pltpu.VMEM((turns, 2, depth, cols), jnp.bfloat16),
            pltpu.VMEM((turns, rows, cols), f32),
            dma((3,)), dma((turns,)), dma((turns,)), dma((turns,)), dma((turns,)),
            dma((devices,)), dma((devices,)),
        ],
        compiler_params=pltpu.CompilerParams(
            collective_id=0, has_side_effects=True, vmem_limit_bytes=40 * 2**20
        ),
        name="fields",
    )(permittivity, conductivity, e_field, h_field, material)


def image_kernel(
    shift, factor, near, table_y, table_x, mask, second, first, spread, tall, spec, total
):
    pols, order = near.shape[0], table_x.shape[0]
    window, coarse = mask.shape[0], spread.shape[1]
    for p in range(pols):
        half = jnp.dot(near[p], table_y[...], precision=HIGHEST, preferred_element_type=jnp.float32)
        real, imag = half[:, :order], half[:, order:]
        both = jnp.concatenate(
            (jnp.concatenate((real, imag), axis=1), jnp.concatenate((imag, -real), axis=1)), axis=0
        )
        value = jnp.dot(table_x[...], both, precision=HIGHEST, preferred_element_type=jnp.float32)
        value = value.astype(jnp.bfloat16).astype(jnp.float32)
        for t in range(spec.shape[1]):
            spec[p, t] = value[:, t * window:(t + 1) * window]
    total[...] = jnp.zeros_like(total)
    keep = mask[...].astype(jnp.float32)

    def add(s, carry):
        a, b = shift[s, 0], shift[s, 1]
        turn = lax.rem(order - b, order)
        pieces = []
        for p in range(pols):
            parts = []
            for k in range(2):
                strip = jnp.concatenate(
                    [
                        spec[p, t, pl.ds(a, window), :]
                        for t in range(k * order // window, (k + 1) * order // window)
                    ],
                    axis=1,
                )
                parts.append(pltpu.roll(strip, turn, 1)[:, :window] * keep)
            pieces.append(jnp.concatenate(parts, axis=1))
        cut = jnp.concatenate(pieces, axis=0).astype(jnp.bfloat16)
        half = jnp.dot(cut, second[...], preferred_element_type=jnp.float32).astype(jnp.bfloat16)
        sides = []
        for p in range(pols):
            part = half[p * window:(p + 1) * window]
            sides.append(jnp.concatenate((part[:, :coarse], part[:, coarse:]), axis=0))
        field = jnp.dot(
            first[...], jnp.concatenate(sides, axis=1), preferred_element_type=jnp.float32
        )
        power = field * field
        power = power[:coarse] + power[coarse:]
        power = sum(power[:, p * coarse:(p + 1) * coarse] for p in range(pols))
        total[...] += factor[s] * power
        return carry

    lax.fori_loop(0, shift.shape[0], add, 0)
    tall[...] = jnp.dot(
        spread[...], total[...], precision=HIGHEST, preferred_element_type=jnp.float32
    ).astype(jnp.bfloat16).reshape(tall.shape)


def run_image(src_shift, factors, near, pupil_mask, devices):
    rows_all, cols_all = near.shape[1], near.shape[2]
    table_y, table_x = spectrum_tables(rows_all, cols_all, K)
    second, first, spread = image_tables(PW, IMG)
    tall = pl.pallas_call(
        image_kernel,
        out_shape=jax.ShapeDtypeStruct((IMG, IMG // 2), jnp.bfloat16),
        in_specs=[SMEM, SMEM] + [VMEM] * 7,
        out_specs=VMEM,
        scratch_shapes=[
            pltpu.VMEM((2, 2 * K // PW, K, PW), jnp.float32),
            pltpu.VMEM((IMG // 2, IMG // 2), jnp.float32),
        ],
        compiler_params=pltpu.CompilerParams(vmem_limit_bytes=40 * 2**20),
        name="sources",
    )(src_shift, factors, near, table_y, table_x, pupil_mask, second, first, spread)
    return tall.reshape(devices, IMG // devices, IMG // 2), spread


def reduce_kernel(nx, ny, tall, spread, image, got, send, recv):
    devices = nx * ny
    me = lax.axis_index("gx") * ny + lax.axis_index("gy")
    greet_all(nx, ny, me)

    def copy(step, other):
        return pltpu.make_async_remote_copy(
            src_ref=tall.at[other], dst_ref=got.at[step], send_sem=send.at[step],
            recv_sem=recv.at[step], device_id=(other // ny, lax.rem(other, ny)), device_id_type=MESH,
        )

    def push(step, carry):
        copy(step, lax.rem(me + step, devices)).start()
        return carry

    lax.fori_loop(1, devices, push, 0)

    def take(step, total):
        arrived = copy(step, lax.rem(me + step, devices))
        arrived.wait_recv()
        arrived.wait_send()
        return total + got[step].astype(jnp.float32)

    owned = lax.fori_loop(1, devices, take, tall[me].astype(jnp.float32))
    image[...] = jnp.dot(owned, spread[...], precision=HIGHEST, preferred_element_type=jnp.float32)


def run_reduce(tall, spread, nx, ny):
    devices = nx * ny
    return pl.pallas_call(
        functools.partial(reduce_kernel, nx, ny),
        out_shape=jax.ShapeDtypeStruct((tall.shape[1], spread.shape[0]), jnp.float32),
        in_specs=[VMEM, VMEM],
        out_specs=VMEM,
        scratch_shapes=[
            pltpu.VMEM(tall.shape, jnp.bfloat16),
            pltpu.SemaphoreType.DMA((devices,)),
            pltpu.SemaphoreType.DMA((devices,)),
        ],
        compiler_params=pltpu.CompilerParams(
            collective_id=1, has_side_effects=True, vmem_limit_bytes=40 * 2**20
        ),
        name="reduce",
    )(tall, np.ascontiguousarray(spread.T))


def local(
    e_field, h_field, material, permittivity, conductivity, src_shift, src_weight, pupil_mask
):
    nx, ny = lax.axis_size("gx"), lax.axis_size("gy")
    devices = nx * ny
    e, h, near = run_fields(e_field, h_field, material, permittivity, conductivity, nx, ny)
    factors = src_weight / (src_shift.shape[0] * devices)
    tall, spread = run_image(src_shift, factors, near, pupil_mask, devices)
    image = run_reduce(tall, spread, nx, ny)
    return (image, e, h)


def solution(mesh):
    return jax.shard_map(
        local,
        mesh=mesh,
        in_specs=(
            P(None, None, "gx", "gy"),
            P(None, None, "gx", "gy"),
            P(None, "gx", "gy"),
            P(),
            P(),
            P(("gx", "gy"), None),
            P(("gx", "gy")),
            P(),
        ),
        out_specs=(P(("gx", "gy"), None), P(None, None, "gx", "gy"), P(None, None, "gx", "gy")),
        check_vma=False,
    )
```

```python
import functools

import jax
import jax.numpy as jnp
import numpy as np
from jax import lax
from jax.experimental import pallas as pl
from jax.experimental.pallas import tpu as pltpu
from jax.sharding import PartitionSpec as P

STEPS = 4
K = 256
PW = 128
IMG = 512
COURANT = 0.5
MESH = pl.DeviceIdType.MESH
HIGHEST = lax.Precision.HIGHEST
VMEM = pl.BlockSpec(memory_space=pltpu.VMEM)
SMEM = pl.BlockSpec(memory_space=pltpu.SMEM)
HBM = pl.BlockSpec(memory_space=pltpu.HBM)
CHUNK = 8


def spectrum_tables(rows_all, cols_all, order):
    freqs = np.arange(order) - order // 2
    phase_y = 2.0 * np.pi * np.mod(np.arange(cols_all)[:, None] * freqs[None, :], cols_all) / cols_all
    table_y = np.concatenate((np.cos(phase_y), -np.sin(phase_y)), axis=1)
    phase_x = 2.0 * np.pi * np.mod(freqs[:, None] * np.arange(rows_all)[None, :], rows_all) / rows_all
    table_x = np.concatenate((np.cos(phase_x), np.sin(phase_x)), axis=1) / np.sqrt(rows_all * cols_all)
    return table_y.astype(np.float32), table_x.astype(np.float32)


def image_tables(window, pixels):
    coarse = pixels // 2
    offsets = np.arange(window) - window // 2
    phase = 2.0 * np.pi * np.mod(offsets[:, None] * np.arange(coarse)[None, :], coarse) / coarse
    cosine, sine = np.cos(phase), np.sin(phase)
    second = np.block([[cosine, sine], [-sine, cosine]])
    first = np.block([[cosine.T, -sine.T], [sine.T, cosine.T]]) / window
    gaps = np.arange(pixels)[:, None] - 2 * np.arange(coarse)[None, :]
    spread = np.ones(gaps.shape)
    for order in range(1, coarse // 2):
        spread += 2.0 * np.cos(2.0 * np.pi * np.mod(order * gaps, pixels) / pixels)
    spread += np.cos(np.pi * gaps / 2.0)
    spread = spread / coarse
    return second.astype(jnp.bfloat16), first.astype(jnp.bfloat16), spread.astype(np.float32)


def greet_all(nx, ny, me):
    barrier = pltpu.get_barrier_semaphore()

    def greet(step, carry):
        other = lax.rem(me + step, nx * ny)
        pl.semaphore_signal(
            barrier, inc=1, device_id=(other // ny, lax.rem(other, ny)), device_id_type=MESH
        )
        return carry

    lax.fori_loop(1, nx * ny, greet, 0)
    pl.semaphore_wait(barrier, nx * ny - 1)


def fields_kernel(
    nx, ny, perm, cond, e_in, h_in, mat_in, e_out, h_out, near,
    e, h, mat, keep, drive, edge_x, face_x, face_y, got_x, got_y, in_sem, x_send, x_recv, y_send, y_recv,
    n_send, n_recv,
):
    depth = mat.shape[0]
    rows, cols = mat.shape[1], mat.shape[2]
    gx, gy = lax.axis_index("gx"), lax.axis_index("gy")
    me = gx * ny + gy
    loads = (
        pltpu.make_async_copy(e_in, e.at[:, pl.ds(0, depth)], in_sem.at[0]),
        pltpu.make_async_copy(h_in, h.at[:, pl.ds(1, depth)], in_sem.at[1]),
        pltpu.make_async_copy(mat_in, mat, in_sem.at[2]),
    )
    for load in loads:
        load.start()
    got_x[...] = jnp.zeros_like(got_x)
    got_y[...] = jnp.zeros_like(got_y)
    greet_all(nx, ny, me)
    zero = jnp.zeros((rows, cols), jnp.float32)
    for c in range(3):
        e[c, depth] = zero
        h[c, 0] = zero
    lane = lax.broadcasted_iota(jnp.int32, (rows, cols), 1)
    lane3 = lax.broadcasted_iota(jnp.int32, (CHUNK, rows, cols), 2)
    row3 = lax.broadcasted_iota(jnp.int32, (CHUNK, rows, cols), 1)
    keeps, drives = [], []
    for m in range(perm.shape[0]):
        loss = cond[m] / (2.0 * perm[m])
        keeps.append((1.0 - loss) / (1.0 + loss))
        drives.append(COURANT / (perm[m] * (1.0 + loss)))

    def x_copy(turn):
        to = gx - 1 if turn % 2 == 0 else gx + 1
        return pltpu.make_async_remote_copy(
            src_ref=face_x.at[turn], dst_ref=got_x.at[turn], send_sem=x_send.at[turn],
            recv_sem=x_recv.at[turn], device_id=(to, gy), device_id_type=MESH,
        )

    def y_copy(turn):
        to = gy - 1 if turn % 2 == 0 else gy + 1
        return pltpu.make_async_remote_copy(
            src_ref=face_y.at[turn], dst_ref=got_y.at[turn], send_sem=y_send.at[turn],
            recv_sem=y_recv.at[turn], device_id=(gx, to), device_id_type=MESH,
        )

    def sends(turn):
        if turn % 2 == 0:
            return gx > 0, gy > 0
        return gx < nx - 1, gy < ny - 1

    def gets(turn):
        if turn % 2 == 0:
            return gx < nx - 1, gy < ny - 1
        return gx > 0, gy > 0

    def start(turn):
        field, base, edge, first, second = (e, 0, 0, 0, 2) if turn % 2 == 0 else (h, 1, cols - 1, 0, 2)
        at_row = 0 if turn % 2 == 0 else rows - 1
        x_to, y_to = sends(turn)
        for k, c in enumerate((1, 2)):
            face_x[turn, k] = field[c, pl.ds(base, depth), at_row, :].astype(jnp.bfloat16)

        @pl.when(x_to)
        def _():
            x_copy(turn).start()

        face = zero
        for k, c in enumerate((first, second)):
            for z in range(depth):
                spot = k * depth + z
                moved = pltpu.roll(field[c, base + z], (spot - edge) % cols, 1)
                face = jnp.where(lane == spot, moved, face)
        face_y[turn] = face

        @pl.when(y_to)
        def _():
            y_copy(turn).start()

    def arrive(turn):
        x_from, y_from = gets(turn)

        @pl.when(y_from)
        def _():
            y_copy(turn).wait_recv()

        @pl.when(x_from)
        def _():
            x_copy(turn).wait_recv()

    def column(face, first, shift):
        return jnp.stack([pltpu.roll(face, (shift - first - z) % cols, 1) for z in range(CHUNK)])

    def magnetic(turn):
        face = got_y[turn]
        edge_x[...] = got_x[turn].astype(jnp.float32)
        last_row, last_lane = row3 == rows - 1, lane3 == cols - 1
        for base in range(0, depth, CHUNK):
            here, next_z = pl.ds(base, CHUNK), pl.ds(base + 1, CHUNK)
            ex, ey, ez = e[0, here], e[1, here], e[2, here]
            ex_z, ey_z = e[0, next_z], e[1, next_z]
            ex_f = column(face, base, cols - 1)
            ez_f = column(face, depth + base, cols - 1)
            ey_x = jnp.where(last_row, edge_x[0, here, :][:, None, :], pltpu.roll(ey, rows - 1, 1))
            ez_x = jnp.where(last_row, edge_x[1, here, :][:, None, :], pltpu.roll(ez, rows - 1, 1))
            ex_y = jnp.where(last_lane, ex_f, pltpu.roll(ex, cols - 1, 2))
            ez_y = jnp.where(last_lane, ez_f, pltpu.roll(ez, cols - 1, 2))
            new_x = h[0, next_z] - COURANT * (ez_y - ez - (ey_z - ey))
            new_y = h[1, next_z] - COURANT * (ex_z - ex - (ez_x - ez))
            new_z = h[2, next_z] - COURANT * (ey_x - ey - (ex_y - ex))
            h[0, next_z] = new_x
            h[1, next_z] = new_y
            h[2, next_z] = new_z

    def electric(turn):
        face = got_y[turn]
        edge_x[...] = got_x[turn].astype(jnp.float32)
        first_row, first_lane = row3 == 0, lane3 == 0
        for base in range(0, depth, CHUNK):
            here, next_z = pl.ds(base, CHUNK), pl.ds(base + 1, CHUNK)
            hx, hy, hz = h[0, next_z], h[1, next_z], h[2, next_z]
            hx_z, hy_z = h[0, here], h[1, here]
            hx_f = column(face, base, 0)
            hz_f = column(face, depth + base, 0)
            hy_x = jnp.where(first_row, edge_x[0, here, :][:, None, :], pltpu.roll(hy, 1, 1))
            hz_x = jnp.where(first_row, edge_x[1, here, :][:, None, :], pltpu.roll(hz, 1, 1))
            hx_y = jnp.where(first_lane, hx_f, pltpu.roll(hx, 1, 2))
            hz_y = jnp.where(first_lane, hz_f, pltpu.roll(hz, 1, 2))
            kept, driven = keep[here], drive[here]
            new_x = kept * e[0, here] + driven * (hz - hz_y - (hy - hy_z))
            new_y = kept * e[1, here] + driven * (hx - hx_z - (hz - hz_x))
            new_z = kept * e[2, here] + driven * (hy - hy_x - (hx - hx_y))
            e[0, here] = new_x
            e[1, here] = new_y
            e[2, here] = new_z

    loads[0].wait()
    start(0)
    loads[2].wait()

    for base in range(0, depth, CHUNK):
        index = mat[base:base + CHUNK]
        kept, driven = jnp.zeros_like(index, jnp.float32), jnp.zeros_like(index, jnp.float32)
        for m in range(len(keeps)):
            chosen = index == m
            kept = jnp.where(chosen, keeps[m], kept)
            driven = jnp.where(chosen, drives[m], driven)
        keep[base:base + CHUNK] = kept
        drive[base:base + CHUNK] = driven

    loads[1].wait()
    for turn in range(2 * STEPS):
        if turn:
            start(turn)
        arrive(turn)
        if turn % 2 == 0:
            magnetic(turn)
        else:
            electric(turn)

    store_h = pltpu.make_async_copy(h.at[:, pl.ds(1, depth)], h_out, in_sem.at[1])
    store_e = pltpu.make_async_copy(e.at[:, pl.ds(0, depth)], e_out, in_sem.at[0])
    store_h.start()
    store_e.start()

    def spot(index):
        x_at = pl.multiple_of((index // ny) * rows, rows)
        y_at = pl.multiple_of(lax.rem(index, ny) * cols, cols)
        return near.at[:, pl.ds(x_at, rows), pl.ds(y_at, cols)]

    def near_copy(step, other, place):
        return pltpu.make_async_remote_copy(
            src_ref=e.at[pl.ds(0, 2), depth - 1], dst_ref=spot(place), send_sem=n_send.at[step],
            recv_sem=n_recv.at[step], device_id=(other // ny, lax.rem(other, ny)), device_id_type=MESH,
        )

    def push(step, carry):
        near_copy(step, lax.rem(me + step, nx * ny), me).start()
        return carry

    lax.fori_loop(1, nx * ny, push, 0)
    own = pltpu.make_async_copy(e.at[pl.ds(0, 2), depth - 1], spot(me), n_send.at[0])
    own.start()
    own.wait()

    def take(step, carry):
        copy = near_copy(
            step, lax.rem(me + step, nx * ny), lax.rem(me - step + nx * ny, nx * ny)
        )
        copy.wait_recv()
        copy.wait_send()
        return carry

    lax.fori_loop(1, nx * ny, take, 0)
    for turn in range(2 * STEPS):
        x_to, y_to = sends(turn)

        @pl.when(x_to)
        def _():
            x_copy(turn).wait_send()

        @pl.when(y_to)
        def _():
            y_copy(turn).wait_send()

    store_h.wait()
    store_e.wait()


def run_fields(e_field, h_field, material, permittivity, conductivity, nx, ny):
    _, depth, rows, cols = e_field.shape
    devices, turns = nx * ny, 2 * STEPS
    f32, dma = jnp.float32, pltpu.SemaphoreType.DMA
    return pl.pallas_call(
        functools.partial(fields_kernel, nx, ny),
        out_shape=(
            jax.ShapeDtypeStruct(e_field.shape, f32),
            jax.ShapeDtypeStruct(h_field.shape, f32),
            jax.ShapeDtypeStruct((2, rows * nx, cols * ny), f32),
        ),
        in_specs=[SMEM, SMEM, HBM, HBM, HBM],
        out_specs=(HBM, HBM, VMEM),
        scratch_shapes=[
            pltpu.VMEM((3, depth + 1, rows, cols), f32),
            pltpu.VMEM((3, depth + 1, rows, cols), f32),
            pltpu.VMEM((depth, rows, cols), jnp.int32),
            pltpu.VMEM((depth, rows, cols), f32),
            pltpu.VMEM((depth, rows, cols), f32),
            pltpu.VMEM((2, depth, cols), f32),
            pltpu.VMEM((turns, 2, depth, cols), jnp.bfloat16),
            pltpu.VMEM((turns, rows, cols), f32),
            pltpu.VMEM((turns, 2, depth, cols), jnp.bfloat16),
            pltpu.VMEM((turns, rows, cols), f32),
            dma((3,)), dma((turns,)), dma((turns,)), dma((turns,)), dma((turns,)),
            dma((devices,)), dma((devices,)),
        ],
        compiler_params=pltpu.CompilerParams(
            collective_id=0, has_side_effects=True, vmem_limit_bytes=61 * 2**20
        ),
        name="fields",
    )(permittivity, conductivity, e_field, h_field, material)


def image_kernel(
    sources, shift, weight, e_in, h_in, near, table_y, table_x, mask, second, first, spread, tall, e_out, h_out, spec, total,
    sem,
):
    moves = (
        pltpu.make_async_copy(e_in, e_out, sem.at[0]),
        pltpu.make_async_copy(h_in, h_out, sem.at[1]),
    )
    for move in moves:
        move.start()
    pols, order = near.shape[0], table_x.shape[0]
    window, coarse = mask.shape[0], spread.shape[1]
    for p in range(pols):
        half = jnp.dot(near[p], table_y[...], precision=HIGHEST, preferred_element_type=jnp.float32)
        real, imag = half[:, :order], half[:, order:]
        both = jnp.concatenate(
            (jnp.concatenate((real, imag), axis=1), jnp.concatenate((imag, -real), axis=1)), axis=0
        )
        value = jnp.dot(table_x[...], both, precision=HIGHEST, preferred_element_type=jnp.float32)
        value = value.astype(jnp.bfloat16).astype(jnp.float32)
        for t in range(spec.shape[1]):
            spec[p, t] = value[:, t * window:(t + 1) * window]
    total[...] = jnp.zeros_like(total)
    keep = mask[...].astype(jnp.float32)

    def add(s, carry):
        a, b = shift[s, 0], shift[s, 1]
        turn = lax.rem(order - b, order)
        pieces = []
        for p in range(pols):
            parts = []
            for k in range(2):
                strip = jnp.concatenate(
                    [
                        spec[p, t, pl.ds(a, window), :]
                        for t in range(k * order // window, (k + 1) * order // window)
                    ],
                    axis=1,
                )
                parts.append(pltpu.roll(strip, turn, 1)[:, :window] * keep)
            pieces.append(jnp.concatenate(parts, axis=1))
        cut = jnp.concatenate(pieces, axis=0).astype(jnp.bfloat16)
        half = jnp.dot(cut, second[...], preferred_element_type=jnp.float32).astype(jnp.bfloat16)
        sides = []
        for p in range(pols):
            part = half[p * window:(p + 1) * window]
            sides.append(jnp.concatenate((part[:, :coarse], part[:, coarse:]), axis=0))
        field = jnp.dot(
            first[...], jnp.concatenate(sides, axis=1), preferred_element_type=jnp.float32
        )
        power = field * field
        power = power[:coarse] + power[coarse:]
        power = sum(power[:, p * coarse:(p + 1) * coarse] for p in range(pols))
        total[...] += weight[s] * (1.0 / sources) * power
        return carry

    lax.fori_loop(0, shift.shape[0], add, 0)
    tall[...] = jnp.dot(
        spread[...], total[...], precision=HIGHEST, preferred_element_type=jnp.float32
    ).astype(jnp.bfloat16).reshape(tall.shape)
    for move in moves:
        move.wait()


def run_image(src_shift, src_weight, e, h, near, pupil_mask, devices):
    rows_all, cols_all = near.shape[1], near.shape[2]
    table_y, table_x = spectrum_tables(rows_all, cols_all, K)
    second, first, spread = image_tables(PW, IMG)
    tall, e, h = pl.pallas_call(
        functools.partial(image_kernel, src_shift.shape[0] * devices),
        out_shape=(
            jax.ShapeDtypeStruct((IMG, IMG // 2), jnp.bfloat16),
            jax.ShapeDtypeStruct(e.shape, e.dtype),
            jax.ShapeDtypeStruct(h.shape, h.dtype),
        ),
        in_specs=[SMEM, SMEM, HBM, HBM] + [VMEM] * 7,
        out_specs=(VMEM, HBM, HBM),
        scratch_shapes=[
            pltpu.VMEM((2, 2 * K // PW, K, PW), jnp.float32),
            pltpu.VMEM((IMG // 2, IMG // 2), jnp.float32),
            pltpu.SemaphoreType.DMA((2,)),
        ],
        compiler_params=pltpu.CompilerParams(vmem_limit_bytes=60 * 2**20),
        name="sources",
    )(src_shift, src_weight, e, h, near, table_y, table_x, pupil_mask, second, first, spread)
    return tall.reshape(devices, IMG // devices, IMG // 2), spread, e, h


def reduce_kernel(nx, ny, tall, spread, image, got, send, recv):
    devices = nx * ny
    me = lax.axis_index("gx") * ny + lax.axis_index("gy")
    greet_all(nx, ny, me)

    def copy(step, other):
        return pltpu.make_async_remote_copy(
            src_ref=tall.at[other], dst_ref=got.at[step], send_sem=send.at[step],
            recv_sem=recv.at[step], device_id=(other // ny, lax.rem(other, ny)), device_id_type=MESH,
        )

    def push(step, carry):
        copy(step, lax.rem(me + step, devices)).start()
        return carry

    lax.fori_loop(1, devices, push, 0)

    def take(step, total):
        arrived = copy(step, lax.rem(me + step, devices))
        arrived.wait_recv()
        arrived.wait_send()
        return total + got[step].astype(jnp.float32)

    owned = lax.fori_loop(1, devices, take, tall[me].astype(jnp.float32))
    image[...] = jnp.dot(owned, spread[...], precision=HIGHEST, preferred_element_type=jnp.float32)


def run_reduce(tall, spread, nx, ny):
    devices = nx * ny
    return pl.pallas_call(
        functools.partial(reduce_kernel, nx, ny),
        out_shape=jax.ShapeDtypeStruct((tall.shape[1], spread.shape[0]), jnp.float32),
        in_specs=[VMEM, VMEM],
        out_specs=VMEM,
        scratch_shapes=[
            pltpu.VMEM(tall.shape, jnp.bfloat16),
            pltpu.SemaphoreType.DMA((devices,)),
            pltpu.SemaphoreType.DMA((devices,)),
        ],
        compiler_params=pltpu.CompilerParams(
            collective_id=1, has_side_effects=True, vmem_limit_bytes=40 * 2**20
        ),
        name="reduce",
    )(tall, np.ascontiguousarray(spread.T))


def local(
    e_field, h_field, material, permittivity, conductivity, src_shift, src_weight, pupil_mask
):
    nx, ny = lax.axis_size("gx"), lax.axis_size("gy")
    devices = nx * ny
    e, h, near = run_fields(e_field, h_field, material, permittivity, conductivity, nx, ny)
    tall, spread, e, h = run_image(src_shift, src_weight, e, h, near, pupil_mask, devices)
    image = run_reduce(tall, spread, nx, ny)
    return (image, e, h)


def solution(mesh):
    return jax.shard_map(
        local,
        mesh=mesh,
        in_specs=(
            P(None, None, "gx", "gy"),
            P(None, None, "gx", "gy"),
            P(None, "gx", "gy"),
            P(),
            P(),
            P(("gx", "gy"), None),
            P(("gx", "gy")),
            P(),
        ),
        out_specs=(P(("gx", "gy"), None), P(None, None, "gx", "gy"), P(None, None, "gx", "gy")),
        check_vma=False,
    )
```

```python
import functools

import jax
import jax.numpy as jnp
import numpy as np
from jax import lax
from jax.experimental import pallas as pl
from jax.experimental.pallas import tpu as pltpu
from jax.sharding import PartitionSpec as P

STEPS = 4
K = 256
PW = 128
IMG = 512
COURANT = 0.5
MESH = pl.DeviceIdType.MESH
HIGHEST = lax.Precision.HIGHEST
VMEM = pl.BlockSpec(memory_space=pltpu.VMEM)
SMEM = pl.BlockSpec(memory_space=pltpu.SMEM)
HBM = pl.BlockSpec(memory_space=pltpu.HBM)
CHUNK = 8
FIELDS_MIB = 60


def spectrum_tables(rows_all, cols_all, order):
    freqs = np.arange(order) - order // 2
    phase_y = 2.0 * np.pi * np.mod(np.arange(cols_all)[:, None] * freqs[None, :], cols_all) / cols_all
    table_y = np.concatenate((np.cos(phase_y), -np.sin(phase_y)), axis=1)
    phase_x = 2.0 * np.pi * np.mod(freqs[:, None] * np.arange(rows_all)[None, :], rows_all) / rows_all
    table_x = np.concatenate((np.cos(phase_x), np.sin(phase_x)), axis=1) / np.sqrt(rows_all * cols_all)
    return table_y.astype(np.float32), table_x.astype(np.float32)


def image_tables(window, pixels):
    coarse = pixels // 2
    offsets = np.arange(window) - window // 2
    phase = 2.0 * np.pi * np.mod(offsets[:, None] * np.arange(coarse)[None, :], coarse) / coarse
    cosine, sine = np.cos(phase), np.sin(phase)
    second = np.block([[cosine, sine], [-sine, cosine]])
    first = np.block([[cosine.T, -sine.T], [sine.T, cosine.T]]) / window
    gaps = np.arange(pixels)[:, None] - 2 * np.arange(coarse)[None, :]
    spread = np.ones(gaps.shape)
    for order in range(1, coarse // 2):
        spread += 2.0 * np.cos(2.0 * np.pi * np.mod(order * gaps, pixels) / pixels)
    spread += np.cos(np.pi * gaps / 2.0)
    spread = spread / coarse
    return second.astype(jnp.bfloat16), first.astype(jnp.bfloat16), spread.astype(np.float32)


def greet_all(nx, ny, me):
    barrier = pltpu.get_barrier_semaphore()

    def greet(step, carry):
        other = lax.rem(me + step, nx * ny)
        pl.semaphore_signal(
            barrier, inc=1, device_id=(other // ny, lax.rem(other, ny)), device_id_type=MESH
        )
        return carry

    lax.fori_loop(1, nx * ny, greet, 0)
    pl.semaphore_wait(barrier, nx * ny - 1)


def fields_kernel(
    nx, ny, perm, cond, e_in, h_in, mat_in, e, h, near,
    mat, keep, drive, edge_x, face_x, face_y, got_x, got_y, in_sem, x_send, x_recv, y_send, y_recv,
    n_send, n_recv,
):
    depth = mat.shape[0]
    rows, cols = mat.shape[1], mat.shape[2]
    gx, gy = lax.axis_index("gx"), lax.axis_index("gy")
    me = gx * ny + gy
    loads = (
        pltpu.make_async_copy(e_in, e, in_sem.at[0]),
        pltpu.make_async_copy(h_in, h, in_sem.at[1]),
        pltpu.make_async_copy(mat_in, mat, in_sem.at[2]),
    )
    for load in loads:
        load.start()
    got_x[...] = jnp.zeros_like(got_x)
    got_y[...] = jnp.zeros_like(got_y)
    greet_all(nx, ny, me)
    zero = jnp.zeros((rows, cols), jnp.float32)
    lane = lax.broadcasted_iota(jnp.int32, (rows, cols), 1)
    lane3 = lax.broadcasted_iota(jnp.int32, (CHUNK, rows, cols), 2)
    row3 = lax.broadcasted_iota(jnp.int32, (CHUNK, rows, cols), 1)
    keeps, drives = [], []
    for m in range(perm.shape[0]):
        loss = cond[m] / (2.0 * perm[m])
        keeps.append((1.0 - loss) / (1.0 + loss))
        drives.append(COURANT / (perm[m] * (1.0 + loss)))

    def x_copy(turn):
        to = gx - 1 if turn % 2 == 0 else gx + 1
        return pltpu.make_async_remote_copy(
            src_ref=face_x.at[turn], dst_ref=got_x.at[turn], send_sem=x_send.at[turn],
            recv_sem=x_recv.at[turn], device_id=(to, gy), device_id_type=MESH,
        )

    def y_copy(turn):
        to = gy - 1 if turn % 2 == 0 else gy + 1
        return pltpu.make_async_remote_copy(
            src_ref=face_y.at[turn], dst_ref=got_y.at[turn], send_sem=y_send.at[turn],
            recv_sem=y_recv.at[turn], device_id=(gx, to), device_id_type=MESH,
        )

    def sends(turn):
        if turn % 2 == 0:
            return gx > 0, gy > 0
        return gx < nx - 1, gy < ny - 1

    def gets(turn):
        if turn % 2 == 0:
            return gx < nx - 1, gy < ny - 1
        return gx > 0, gy > 0

    def start(turn):
        field, edge, first, second = (e, 0, 0, 2) if turn % 2 == 0 else (h, cols - 1, 0, 2)
        at_row = 0 if turn % 2 == 0 else rows - 1
        x_to, y_to = sends(turn)
        for k, c in enumerate((1, 2)):
            face_x[turn, k] = field[c, :, at_row, :].astype(jnp.bfloat16)

        @pl.when(x_to)
        def _():
            x_copy(turn).start()

        face = zero
        for k, c in enumerate((first, second)):
            for z in range(depth):
                spot = k * depth + z
                moved = pltpu.roll(field[c, z], (spot - edge) % cols, 1)
                face = jnp.where(lane == spot, moved, face)
        face_y[turn] = face

        @pl.when(y_to)
        def _():
            y_copy(turn).start()

    def arrive(turn):
        x_from, y_from = gets(turn)

        @pl.when(y_from)
        def _():
            y_copy(turn).wait_recv()

        @pl.when(x_from)
        def _():
            x_copy(turn).wait_recv()

    def column(face, first, shift):
        return jnp.stack([pltpu.roll(face, (shift - first - z) % cols, 1) for z in range(CHUNK)])

    def above(field, c, base):
        end = min(base + 1 + CHUNK, depth)
        value = field[c, base + 1:end]
        if end == depth:
            value = jnp.concatenate((value, zero[None]), axis=0)
        return value

    def below(field, c, base):
        if base:
            return field[c, base - 1:base - 1 + CHUNK]
        return jnp.concatenate((zero[None], field[c, :CHUNK - 1]), axis=0)

    def magnetic(turn):
        face = got_y[turn]
        edge_x[...] = got_x[turn].astype(jnp.float32)
        last_row, last_lane = row3 == rows - 1, lane3 == cols - 1
        for base in range(0, depth, CHUNK):
            here = pl.ds(base, CHUNK)
            ex, ey, ez = e[0, here], e[1, here], e[2, here]
            ex_z, ey_z = above(e, 0, base), above(e, 1, base)
            ex_f = column(face, base, cols - 1)
            ez_f = column(face, depth + base, cols - 1)
            ey_x = jnp.where(last_row, edge_x[0, here, :][:, None, :], pltpu.roll(ey, rows - 1, 1))
            ez_x = jnp.where(last_row, edge_x[1, here, :][:, None, :], pltpu.roll(ez, rows - 1, 1))
            ex_y = jnp.where(last_lane, ex_f, pltpu.roll(ex, cols - 1, 2))
            ez_y = jnp.where(last_lane, ez_f, pltpu.roll(ez, cols - 1, 2))
            new_x = h[0, here] - COURANT * (ez_y - ez - (ey_z - ey))
            new_y = h[1, here] - COURANT * (ex_z - ex - (ez_x - ez))
            new_z = h[2, here] - COURANT * (ey_x - ey - (ex_y - ex))
            h[0, here] = new_x
            h[1, here] = new_y
            h[2, here] = new_z

    def electric(turn):
        face = got_y[turn]
        edge_x[...] = got_x[turn].astype(jnp.float32)
        first_row, first_lane = row3 == 0, lane3 == 0
        for base in range(0, depth, CHUNK):
            here = pl.ds(base, CHUNK)
            hx, hy, hz = h[0, here], h[1, here], h[2, here]
            hx_z, hy_z = below(h, 0, base), below(h, 1, base)
            hx_f = column(face, base, 0)
            hz_f = column(face, depth + base, 0)
            hy_x = jnp.where(first_row, edge_x[0, here, :][:, None, :], pltpu.roll(hy, 1, 1))
            hz_x = jnp.where(first_row, edge_x[1, here, :][:, None, :], pltpu.roll(hz, 1, 1))
            hx_y = jnp.where(first_lane, hx_f, pltpu.roll(hx, 1, 2))
            hz_y = jnp.where(first_lane, hz_f, pltpu.roll(hz, 1, 2))
            kept, driven = keep[here], drive[here]
            new_x = kept * e[0, here] + driven * (hz - hz_y - (hy - hy_z))
            new_y = kept * e[1, here] + driven * (hx - hx_z - (hz - hz_x))
            new_z = kept * e[2, here] + driven * (hy - hy_x - (hx - hx_y))
            e[0, here] = new_x
            e[1, here] = new_y
            e[2, here] = new_z

    loads[0].wait()
    start(0)
    loads[2].wait()

    for base in range(0, depth, CHUNK):
        index = mat[base:base + CHUNK]
        kept, driven = jnp.zeros_like(index, jnp.float32), jnp.zeros_like(index, jnp.float32)
        for m in range(len(keeps)):
            chosen = index == m
            kept = jnp.where(chosen, keeps[m], kept)
            driven = jnp.where(chosen, drives[m], driven)
        keep[base:base + CHUNK] = kept
        drive[base:base + CHUNK] = driven

    loads[1].wait()
    for turn in range(2 * STEPS):
        if turn:
            start(turn)
        arrive(turn)
        if turn % 2 == 0:
            magnetic(turn)
        else:
            electric(turn)

    def spot(index):
        x_at = pl.multiple_of((index // ny) * rows, rows)
        y_at = pl.multiple_of(lax.rem(index, ny) * cols, cols)
        return near.at[:, pl.ds(x_at, rows), pl.ds(y_at, cols)]

    def near_copy(step, other, place):
        return pltpu.make_async_remote_copy(
            src_ref=e.at[pl.ds(0, 2), depth - 1], dst_ref=spot(place), send_sem=n_send.at[step],
            recv_sem=n_recv.at[step], device_id=(other // ny, lax.rem(other, ny)), device_id_type=MESH,
        )

    def push(step, carry):
        near_copy(step, lax.rem(me + step, nx * ny), me).start()
        return carry

    lax.fori_loop(1, nx * ny, push, 0)
    own = pltpu.make_async_copy(e.at[pl.ds(0, 2), depth - 1], spot(me), n_send.at[0])
    own.start()
    own.wait()

    def take(step, carry):
        copy = near_copy(
            step, lax.rem(me + step, nx * ny), lax.rem(me - step + nx * ny, nx * ny)
        )
        copy.wait_recv()
        copy.wait_send()
        return carry

    lax.fori_loop(1, nx * ny, take, 0)
    for turn in range(2 * STEPS):
        x_to, y_to = sends(turn)

        @pl.when(x_to)
        def _():
            x_copy(turn).wait_send()

        @pl.when(y_to)
        def _():
            y_copy(turn).wait_send()


def run_fields(e_field, h_field, material, permittivity, conductivity, nx, ny):
    _, depth, rows, cols = e_field.shape
    devices, turns = nx * ny, 2 * STEPS
    f32, dma = jnp.float32, pltpu.SemaphoreType.DMA
    return pl.pallas_call(
        functools.partial(fields_kernel, nx, ny),
        out_shape=(
            jax.ShapeDtypeStruct(e_field.shape, f32),
            jax.ShapeDtypeStruct(h_field.shape, f32),
            jax.ShapeDtypeStruct((2, rows * nx, cols * ny), f32),
        ),
        in_specs=[SMEM, SMEM, HBM, HBM, HBM],
        out_specs=(VMEM, VMEM, VMEM),
        scratch_shapes=[
            pltpu.VMEM((depth, rows, cols), jnp.int32),
            pltpu.VMEM((depth, rows, cols), f32),
            pltpu.VMEM((depth, rows, cols), f32),
            pltpu.VMEM((2, depth, cols), f32),
            pltpu.VMEM((turns, 2, depth, cols), jnp.bfloat16),
            pltpu.VMEM((turns, rows, cols), f32),
            pltpu.VMEM((turns, 2, depth, cols), jnp.bfloat16),
            pltpu.VMEM((turns, rows, cols), f32),
            dma((3,)), dma((turns,)), dma((turns,)), dma((turns,)), dma((turns,)),
            dma((devices,)), dma((devices,)),
        ],
        compiler_params=pltpu.CompilerParams(
            collective_id=0, has_side_effects=True, vmem_limit_bytes=FIELDS_MIB * 2**20
        ),
        name="fields",
    )(permittivity, conductivity, e_field, h_field, material)


def image_kernel(
    sources, shift, weight, near, table_y, table_x, mask, second, first, spread, tall, spec, total,
):
    pols, order = near.shape[0], table_x.shape[0]
    window, coarse = mask.shape[0], spread.shape[1]
    for p in range(pols):
        half = jnp.dot(near[p], table_y[...], precision=HIGHEST, preferred_element_type=jnp.float32)
        real, imag = half[:, :order], half[:, order:]
        both = jnp.concatenate(
            (jnp.concatenate((real, imag), axis=1), jnp.concatenate((imag, -real), axis=1)), axis=0
        )
        value = jnp.dot(table_x[...], both, precision=HIGHEST, preferred_element_type=jnp.float32)
        value = value.astype(jnp.bfloat16).astype(jnp.float32)
        for t in range(spec.shape[1]):
            spec[p, t] = value[:, t * window:(t + 1) * window]
    total[...] = jnp.zeros_like(total)
    keep = mask[...].astype(jnp.float32)

    def add(s, carry):
        a, b = shift[s, 0], shift[s, 1]
        turn = lax.rem(order - b, order)
        pieces = []
        for p in range(pols):
            parts = []
            for k in range(2):
                strip = jnp.concatenate(
                    [
                        spec[p, t, pl.ds(a, window), :]
                        for t in range(k * order // window, (k + 1) * order // window)
                    ],
                    axis=1,
                )
                parts.append(pltpu.roll(strip, turn, 1)[:, :window] * keep)
            pieces.append(jnp.concatenate(parts, axis=1))
        cut = jnp.concatenate(pieces, axis=0).astype(jnp.bfloat16)
        half = jnp.dot(cut, second[...], preferred_element_type=jnp.float32).astype(jnp.bfloat16)
        sides = []
        for p in range(pols):
            part = half[p * window:(p + 1) * window]
            sides.append(jnp.concatenate((part[:, :coarse], part[:, coarse:]), axis=0))
        field = jnp.dot(
            first[...], jnp.concatenate(sides, axis=1), preferred_element_type=jnp.float32
        )
        power = field * field
        power = power[:coarse] + power[coarse:]
        power = sum(power[:, p * coarse:(p + 1) * coarse] for p in range(pols))
        total[...] += weight[s] * (1.0 / sources) * power
        return carry

    lax.fori_loop(0, shift.shape[0], add, 0)
    tall[...] = jnp.dot(
        spread[...], total[...], precision=HIGHEST, preferred_element_type=jnp.float32
    ).astype(jnp.bfloat16).reshape(tall.shape)


def run_image(src_shift, src_weight, near, pupil_mask, devices):
    rows_all, cols_all = near.shape[1], near.shape[2]
    table_y, table_x = spectrum_tables(rows_all, cols_all, K)
    second, first, spread = image_tables(PW, IMG)
    tall = pl.pallas_call(
        functools.partial(image_kernel, src_shift.shape[0] * devices),
        out_shape=jax.ShapeDtypeStruct((IMG, IMG // 2), jnp.bfloat16),
        in_specs=[SMEM, SMEM] + [VMEM] * 7,
        out_specs=VMEM,
        scratch_shapes=[
            pltpu.VMEM((2, 2 * K // PW, K, PW), jnp.float32),
            pltpu.VMEM((IMG // 2, IMG // 2), jnp.float32),
        ],
        compiler_params=pltpu.CompilerParams(vmem_limit_bytes=40 * 2**20),
        name="sources",
    )(src_shift, src_weight, near, table_y, table_x, pupil_mask, second, first, spread)
    return tall.reshape(devices, IMG // devices, IMG // 2), spread


def reduce_kernel(nx, ny, tall, spread, image, got, send, recv):
    devices = nx * ny
    me = lax.axis_index("gx") * ny + lax.axis_index("gy")
    greet_all(nx, ny, me)

    def copy(step, other):
        return pltpu.make_async_remote_copy(
            src_ref=tall.at[other], dst_ref=got.at[step], send_sem=send.at[step],
            recv_sem=recv.at[step], device_id=(other // ny, lax.rem(other, ny)), device_id_type=MESH,
        )

    def push(step, carry):
        copy(step, lax.rem(me + step, devices)).start()
        return carry

    lax.fori_loop(1, devices, push, 0)

    def take(step, total):
        arrived = copy(step, lax.rem(me + step, devices))
        arrived.wait_recv()
        arrived.wait_send()
        return total + got[step].astype(jnp.float32)

    owned = lax.fori_loop(1, devices, take, tall[me].astype(jnp.float32))
    image[...] = jnp.dot(owned, spread[...], precision=HIGHEST, preferred_element_type=jnp.float32)


def run_reduce(tall, spread, nx, ny):
    devices = nx * ny
    return pl.pallas_call(
        functools.partial(reduce_kernel, nx, ny),
        out_shape=jax.ShapeDtypeStruct((tall.shape[1], spread.shape[0]), jnp.float32),
        in_specs=[VMEM, VMEM],
        out_specs=VMEM,
        scratch_shapes=[
            pltpu.VMEM(tall.shape, jnp.bfloat16),
            pltpu.SemaphoreType.DMA((devices,)),
            pltpu.SemaphoreType.DMA((devices,)),
        ],
        compiler_params=pltpu.CompilerParams(
            collective_id=1, has_side_effects=True, vmem_limit_bytes=40 * 2**20
        ),
        name="reduce",
    )(tall, np.ascontiguousarray(spread.T))


def local(
    e_field, h_field, material, permittivity, conductivity, src_shift, src_weight, pupil_mask
):
    nx, ny = lax.axis_size("gx"), lax.axis_size("gy")
    devices = nx * ny
    e, h, near = run_fields(e_field, h_field, material, permittivity, conductivity, nx, ny)
    tall, spread = run_image(src_shift, src_weight, near, pupil_mask, devices)
    image = run_reduce(tall, spread, nx, ny)
    return (image, e, h)


def solution(mesh):
    return jax.shard_map(
        local,
        mesh=mesh,
        in_specs=(
            P(None, None, "gx", "gy"),
            P(None, None, "gx", "gy"),
            P(None, "gx", "gy"),
            P(),
            P(),
            P(("gx", "gy"), None),
            P(("gx", "gy")),
            P(),
        ),
        out_specs=(P(("gx", "gy"), None), P(None, None, "gx", "gy"), P(None, None, "gx", "gy")),
        check_vma=False,
    )
```

```python
import functools

import jax
import jax.numpy as jnp
import numpy as np
from jax import lax
from jax.experimental import pallas as pl
from jax.experimental.pallas import tpu as pltpu
from jax.sharding import PartitionSpec as P

STEPS = 4
K = 256
PW = 128
IMG = 512
COURANT = 0.5
MESH = pl.DeviceIdType.MESH
HIGHEST = lax.Precision.HIGHEST
VMEM = pl.BlockSpec(memory_space=pltpu.VMEM)
SMEM = pl.BlockSpec(memory_space=pltpu.SMEM)
HBM = pl.BlockSpec(memory_space=pltpu.HBM)
CHUNK = 8
FIELDS_MIB = 60


def spectrum_tables(rows_all, cols_all, order):
    freqs = np.arange(order) - order // 2
    phase_y = 2.0 * np.pi * np.mod(np.arange(cols_all)[:, None] * freqs[None, :], cols_all) / cols_all
    table_y = np.concatenate((np.cos(phase_y), -np.sin(phase_y)), axis=1)
    phase_x = 2.0 * np.pi * np.mod(freqs[:, None] * np.arange(rows_all)[None, :], rows_all) / rows_all
    table_x = np.concatenate((np.cos(phase_x), np.sin(phase_x)), axis=1) / np.sqrt(rows_all * cols_all)
    return table_y.astype(np.float32), table_x.astype(np.float32)


def image_tables(window, pixels):
    coarse = pixels // 2
    offsets = np.arange(window) - window // 2
    phase = 2.0 * np.pi * np.mod(offsets[:, None] * np.arange(coarse)[None, :], coarse) / coarse
    cosine, sine = np.cos(phase), np.sin(phase)
    second = np.block([[cosine, sine], [-sine, cosine]])
    first = np.block([[cosine.T, -sine.T], [sine.T, cosine.T]]) / window
    gaps = np.arange(pixels)[:, None] - 2 * np.arange(coarse)[None, :]
    spread = np.ones(gaps.shape)
    for order in range(1, coarse // 2):
        spread += 2.0 * np.cos(2.0 * np.pi * np.mod(order * gaps, pixels) / pixels)
    spread += np.cos(np.pi * gaps / 2.0)
    spread = spread / coarse
    return second.astype(jnp.bfloat16), first.astype(jnp.bfloat16), spread.astype(np.float32)


def greet_all(nx, ny, me):
    barrier = pltpu.get_barrier_semaphore()

    def greet(step, carry):
        other = lax.rem(me + step, nx * ny)
        pl.semaphore_signal(
            barrier, inc=1, device_id=(other // ny, lax.rem(other, ny)), device_id_type=MESH
        )
        return carry

    lax.fori_loop(1, nx * ny, greet, 0)
    pl.semaphore_wait(barrier, nx * ny - 1)


def fields_kernel(
    nx, ny, perm, cond, e_in, h_in, mat_in, e, h, near,
    mat, keep, drive, own, edge_x, up_out, low_out, pack_out, up_in, low_in, pack_in, far_row, far_col,
    in_sem, f_send, f_recv, n_send, n_recv,
):
    depth = mat.shape[0]
    rows, cols = mat.shape[1], mat.shape[2]
    gx, gy = lax.axis_index("gx"), lax.axis_index("gy")
    me = gx * ny + gy
    loads = (
        pltpu.make_async_copy(e_in, e, in_sem.at[0]),
        pltpu.make_async_copy(h_in, h, in_sem.at[1]),
        pltpu.make_async_copy(mat_in, mat, in_sem.at[2]),
    )
    for load in loads:
        load.start()
    for landing in (up_in, low_in, pack_in, far_row, far_col):
        landing[...] = jnp.zeros_like(landing)
    greet_all(nx, ny, me)
    zero = jnp.zeros((rows, cols), jnp.float32)
    lane = lax.broadcasted_iota(jnp.int32, (rows, cols), 1)
    lane3 = lax.broadcasted_iota(jnp.int32, (CHUNK, rows, cols), 2)
    row3 = lax.broadcasted_iota(jnp.int32, (CHUNK, rows, cols), 1)
    keeps, drives = [], []
    for m in range(perm.shape[0]):
        loss = cond[m] / (2.0 * perm[m])
        keeps.append((1.0 - loss) / (1.0 + loss))
        drives.append(COURANT / (perm[m] * (1.0 + loss)))

    west, east = gx > 0, gx < nx - 1
    south, north = gy > 0, gy < ny - 1

    def copies(step):
        routes = (
            (east, west, low_out.at[step], low_in.at[step], 1, 0),
            (west, east, up_out.at[step], up_in.at[step], -1, 0),
            (south, north, pack_out.at[step, 0], pack_in.at[step, 0], 0, -1),
            (north, south, pack_out.at[step, pl.ds(1, 3)], pack_in.at[step, pl.ds(1, 3)], 0, 1),
            (
                jnp.logical_and(east, south), jnp.logical_and(west, north),
                low_out.at[step, 0], far_row.at[step], 1, -1,
            ),
            (
                jnp.logical_and(west, north), jnp.logical_and(east, south),
                pack_out.at[step, 3], far_col.at[step], -1, 1,
            ),
        )
        return [
            (
                sends, gets,
                pltpu.make_async_remote_copy(
                    src_ref=src, dst_ref=dst, send_sem=f_send.at[step, kind],
                    recv_sem=f_recv.at[step, kind], device_id=(gx + dx, gy + dy),
                    device_id_type=MESH,
                ),
            )
            for kind, (sends, gets, src, dst, dx, dy) in enumerate(routes)
        ]

    def packed(parts, edge):
        face = zero
        for k, (field, c) in enumerate(parts):
            for z in range(depth):
                spot = k * depth + z
                moved = pltpu.roll(field[c, z], (spot - edge) % cols, 1)
                face = jnp.where(lane == spot, moved, face)
        return face

    def start(step):
        routes = copies(step)

        def go(kind):
            sends, _, copy = routes[kind]

            @pl.when(sends)
            def _():
                copy.start()

        for k, (field, c) in enumerate(((e, 0), (e, 1), (e, 2), (h, 1), (h, 2))):
            low_out[step, k] = field[c, :, rows - 1, :].astype(jnp.bfloat16)
        go(0)
        go(4)
        for k, c in enumerate((1, 2)):
            value = e[c, :, 0, :]
            own[k] = value
            up_out[step, k] = value.astype(jnp.bfloat16)
        go(1)
        pack_out[step, 3] = packed(((e, 1),), cols - 1)
        go(5)
        pack_out[step, 1] = packed(((e, 0), (e, 2)), cols - 1)
        pack_out[step, 2] = packed(((h, 0), (h, 2)), cols - 1)
        go(3)
        pack_out[step, 0] = packed(((e, 0), (e, 2)), 0)
        go(2)

    def arrive(step):
        for _, gets, copy in copies(step):
            @pl.when(gets)
            def _():
                copy.wait_recv()

    def ghosts(step):
        c_x = jnp.where(west, COURANT, 0.0)
        c_y = jnp.where(south, COURANT, 0.0)
        ex, ey, ez, hy, hz = (low_in[step, k].astype(jnp.float32) for k in range(5))
        flat_z = lax.broadcasted_iota(jnp.int32, (depth, cols), 0)
        flat_y = lax.broadcasted_iota(jnp.int32, (depth, cols), 1)
        corner = pltpu.roll(far_row[step].astype(jnp.float32), cols - 1, 1)
        ex_z = jnp.where(flat_z == depth - 1, 0.0, pltpu.roll(ex, depth - 1, 0))
        ex_y = jnp.where(flat_y == cols - 1, corner, pltpu.roll(ex, cols - 1, 1))
        edge_x[0] = hy - c_x * (ex_z - ex - (own[1] - ez))
        edge_x[1] = hz - c_x * (own[0] - ey - (ex_y - ex))
        row = lax.broadcasted_iota(jnp.int32, (rows, cols), 0)
        e_side, h_side, ey_side = pack_in[step, 1], pack_in[step, 2], pack_in[step, 3]
        across = pltpu.roll(pack_out[step, 0] - e_side, depth, 1)
        ey_z = pltpu.roll(ey_side, cols - 1, 1)
        ey_x = jnp.where(
            row == rows - 1, pltpu.roll(far_col[step], rows - 1, 0), pltpu.roll(ey_side, rows - 1, 0)
        )
        turn_x = across - (ey_z - ey_side)
        turn_z = pltpu.roll(ey_x - ey_side, depth, 1) - across
        return h_side - c_y * jnp.where(lane < depth, turn_x, turn_z)

    def column(face, first, shift):
        return jnp.stack([pltpu.roll(face, (shift - first - z) % cols, 1) for z in range(CHUNK)])

    def above(field, c, base):
        end = min(base + 1 + CHUNK, depth)
        value = field[c, base + 1:end]
        if end == depth:
            value = jnp.concatenate((value, zero[None]), axis=0)
        return value

    def below(field, c, base):
        if base:
            return field[c, base - 1:base - 1 + CHUNK]
        return jnp.concatenate((zero[None], field[c, :CHUNK - 1]), axis=0)

    def magnetic(step):
        face = pack_in[step, 0]
        edge_x[...] = up_in[step].astype(jnp.float32)
        last_row, last_lane = row3 == rows - 1, lane3 == cols - 1
        for base in range(0, depth, CHUNK):
            here = pl.ds(base, CHUNK)
            ex, ey, ez = e[0, here], e[1, here], e[2, here]
            ex_z, ey_z = above(e, 0, base), above(e, 1, base)
            ex_f = column(face, base, cols - 1)
            ez_f = column(face, depth + base, cols - 1)
            ey_x = jnp.where(last_row, edge_x[0, here, :][:, None, :], pltpu.roll(ey, rows - 1, 1))
            ez_x = jnp.where(last_row, edge_x[1, here, :][:, None, :], pltpu.roll(ez, rows - 1, 1))
            ex_y = jnp.where(last_lane, ex_f, pltpu.roll(ex, cols - 1, 2))
            ez_y = jnp.where(last_lane, ez_f, pltpu.roll(ez, cols - 1, 2))
            new_x = h[0, here] - COURANT * (ez_y - ez - (ey_z - ey))
            new_y = h[1, here] - COURANT * (ex_z - ex - (ez_x - ez))
            new_z = h[2, here] - COURANT * (ey_x - ey - (ex_y - ex))
            h[0, here] = new_x
            h[1, here] = new_y
            h[2, here] = new_z

    def electric(face):
        first_row, first_lane = row3 == 0, lane3 == 0
        for base in range(0, depth, CHUNK):
            here = pl.ds(base, CHUNK)
            hx, hy, hz = h[0, here], h[1, here], h[2, here]
            hx_z, hy_z = below(h, 0, base), below(h, 1, base)
            hx_f = column(face, base, 0)
            hz_f = column(face, depth + base, 0)
            hy_x = jnp.where(first_row, edge_x[0, here, :][:, None, :], pltpu.roll(hy, 1, 1))
            hz_x = jnp.where(first_row, edge_x[1, here, :][:, None, :], pltpu.roll(hz, 1, 1))
            hx_y = jnp.where(first_lane, hx_f, pltpu.roll(hx, 1, 2))
            hz_y = jnp.where(first_lane, hz_f, pltpu.roll(hz, 1, 2))
            kept, driven = keep[here], drive[here]
            new_x = kept * e[0, here] + driven * (hz - hz_y - (hy - hy_z))
            new_y = kept * e[1, here] + driven * (hx - hx_z - (hz - hz_x))
            new_z = kept * e[2, here] + driven * (hy - hy_x - (hx - hx_y))
            e[0, here] = new_x
            e[1, here] = new_y
            e[2, here] = new_z

    loads[2].wait()

    for base in range(0, depth, CHUNK):
        index = mat[base:base + CHUNK]
        kept, driven = jnp.zeros_like(index, jnp.float32), jnp.zeros_like(index, jnp.float32)
        for m in range(len(keeps)):
            chosen = index == m
            kept = jnp.where(chosen, keeps[m], kept)
            driven = jnp.where(chosen, drives[m], driven)
        keep[base:base + CHUNK] = kept
        drive[base:base + CHUNK] = driven

    loads[1].wait()
    loads[0].wait()
    start(0)
    for step in range(STEPS):
        if step:
            start(step)
        arrive(step)
        magnetic(step)
        electric(ghosts(step))

    def spot(index):
        x_at = pl.multiple_of((index // ny) * rows, rows)
        y_at = pl.multiple_of(lax.rem(index, ny) * cols, cols)
        return near.at[:, pl.ds(x_at, rows), pl.ds(y_at, cols)]

    def near_copy(step, other, place):
        return pltpu.make_async_remote_copy(
            src_ref=e.at[pl.ds(0, 2), depth - 1], dst_ref=spot(place), send_sem=n_send.at[step],
            recv_sem=n_recv.at[step], device_id=(other // ny, lax.rem(other, ny)), device_id_type=MESH,
        )

    def push(step, carry):
        near_copy(step, lax.rem(me + step, nx * ny), me).start()
        return carry

    lax.fori_loop(1, nx * ny, push, 0)
    kept_near = pltpu.make_async_copy(e.at[pl.ds(0, 2), depth - 1], spot(me), n_send.at[0])
    kept_near.start()
    kept_near.wait()

    def take(step, carry):
        copy = near_copy(
            step, lax.rem(me + step, nx * ny), lax.rem(me - step + nx * ny, nx * ny)
        )
        copy.wait_recv()
        copy.wait_send()
        return carry

    lax.fori_loop(1, nx * ny, take, 0)
    for step in range(STEPS):
        for sends, _, copy in copies(step):
            @pl.when(sends)
            def _():
                copy.wait_send()


def run_fields(e_field, h_field, material, permittivity, conductivity, nx, ny):
    _, depth, rows, cols = e_field.shape
    devices = nx * ny
    f32, dma = jnp.float32, pltpu.SemaphoreType.DMA
    return pl.pallas_call(
        functools.partial(fields_kernel, nx, ny),
        out_shape=(
            jax.ShapeDtypeStruct(e_field.shape, f32),
            jax.ShapeDtypeStruct(h_field.shape, f32),
            jax.ShapeDtypeStruct((2, rows * nx, cols * ny), f32),
        ),
        in_specs=[SMEM, SMEM, HBM, HBM, HBM],
        out_specs=(VMEM, VMEM, VMEM),
        scratch_shapes=[
            pltpu.VMEM((depth, rows, cols), jnp.int32),
            pltpu.VMEM((depth, rows, cols), f32),
            pltpu.VMEM((depth, rows, cols), f32),
            pltpu.VMEM((2, depth, cols), f32),
            pltpu.VMEM((2, depth, cols), f32),
            pltpu.VMEM((STEPS, 2, depth, cols), jnp.bfloat16),
            pltpu.VMEM((STEPS, 5, depth, cols), jnp.bfloat16),
            pltpu.VMEM((STEPS, 4, rows, cols), f32),
            pltpu.VMEM((STEPS, 2, depth, cols), jnp.bfloat16),
            pltpu.VMEM((STEPS, 5, depth, cols), jnp.bfloat16),
            pltpu.VMEM((STEPS, 4, rows, cols), f32),
            pltpu.VMEM((STEPS, depth, cols), jnp.bfloat16),
            pltpu.VMEM((STEPS, rows, cols), f32),
            dma((3,)), dma((STEPS, 6)), dma((STEPS, 6)),
            dma((devices,)), dma((devices,)),
        ],
        compiler_params=pltpu.CompilerParams(
            collective_id=0, has_side_effects=True, vmem_limit_bytes=FIELDS_MIB * 2**20
        ),
        name="fields",
    )(permittivity, conductivity, e_field, h_field, material)


def image_kernel(
    sources, shift, weight, near, table_y, table_x, mask, second, first, spread, tall, spec, total,
):
    pols, order = near.shape[0], table_x.shape[0]
    window, coarse = mask.shape[0], spread.shape[1]
    for p in range(pols):
        half = jnp.dot(near[p], table_y[...], precision=HIGHEST, preferred_element_type=jnp.float32)
        real, imag = half[:, :order], half[:, order:]
        both = jnp.concatenate(
            (jnp.concatenate((real, imag), axis=1), jnp.concatenate((imag, -real), axis=1)), axis=0
        )
        value = jnp.dot(table_x[...], both, precision=HIGHEST, preferred_element_type=jnp.float32)
        value = value.astype(jnp.bfloat16).astype(jnp.float32)
        for t in range(spec.shape[1]):
            spec[p, t] = value[:, t * window:(t + 1) * window]
    total[...] = jnp.zeros_like(total)
    keep = mask[...].astype(jnp.float32)

    def add(s, carry):
        a, b = shift[s, 0], shift[s, 1]
        turn = lax.rem(order - b, order)
        pieces = []
        for p in range(pols):
            parts = []
            for k in range(2):
                strip = jnp.concatenate(
                    [
                        spec[p, t, pl.ds(a, window), :]
                        for t in range(k * order // window, (k + 1) * order // window)
                    ],
                    axis=1,
                )
                parts.append(pltpu.roll(strip, turn, 1)[:, :window] * keep)
            pieces.append(jnp.concatenate(parts, axis=1))
        cut = jnp.concatenate(pieces, axis=0).astype(jnp.bfloat16)
        half = jnp.dot(cut, second[...], preferred_element_type=jnp.float32).astype(jnp.bfloat16)
        sides = []
        for p in range(pols):
            part = half[p * window:(p + 1) * window]
            sides.append(jnp.concatenate((part[:, :coarse], part[:, coarse:]), axis=0))
        field = jnp.dot(
            first[...], jnp.concatenate(sides, axis=1), preferred_element_type=jnp.float32
        )
        power = field * field
        power = power[:coarse] + power[coarse:]
        power = sum(power[:, p * coarse:(p + 1) * coarse] for p in range(pols))
        total[...] += weight[s] * (1.0 / sources) * power
        return carry

    lax.fori_loop(0, shift.shape[0], add, 0)
    tall[...] = jnp.dot(
        spread[...], total[...], precision=HIGHEST, preferred_element_type=jnp.float32
    ).astype(jnp.bfloat16).reshape(tall.shape)


def run_image(src_shift, src_weight, near, pupil_mask, devices):
    rows_all, cols_all = near.shape[1], near.shape[2]
    table_y, table_x = spectrum_tables(rows_all, cols_all, K)
    second, first, spread = image_tables(PW, IMG)
    tall = pl.pallas_call(
        functools.partial(image_kernel, src_shift.shape[0] * devices),
        out_shape=jax.ShapeDtypeStruct((IMG, IMG // 2), jnp.bfloat16),
        in_specs=[SMEM, SMEM] + [VMEM] * 7,
        out_specs=VMEM,
        scratch_shapes=[
            pltpu.VMEM((2, 2 * K // PW, K, PW), jnp.float32),
            pltpu.VMEM((IMG // 2, IMG // 2), jnp.float32),
        ],
        compiler_params=pltpu.CompilerParams(vmem_limit_bytes=40 * 2**20),
        name="sources",
    )(src_shift, src_weight, near, table_y, table_x, pupil_mask, second, first, spread)
    return tall.reshape(devices, IMG // devices, IMG // 2), spread


def reduce_kernel(nx, ny, tall, spread, image, got, send, recv):
    devices = nx * ny
    me = lax.axis_index("gx") * ny + lax.axis_index("gy")
    greet_all(nx, ny, me)

    def copy(step, other):
        return pltpu.make_async_remote_copy(
            src_ref=tall.at[other], dst_ref=got.at[step], send_sem=send.at[step],
            recv_sem=recv.at[step], device_id=(other // ny, lax.rem(other, ny)), device_id_type=MESH,
        )

    def push(step, carry):
        copy(step, lax.rem(me + step, devices)).start()
        return carry

    lax.fori_loop(1, devices, push, 0)

    def take(step, total):
        arrived = copy(step, lax.rem(me + step, devices))
        arrived.wait_recv()
        arrived.wait_send()
        return total + got[step].astype(jnp.float32)

    owned = lax.fori_loop(1, devices, take, tall[me].astype(jnp.float32))
    image[...] = jnp.dot(owned, spread[...], precision=HIGHEST, preferred_element_type=jnp.float32)


def run_reduce(tall, spread, nx, ny):
    devices = nx * ny
    return pl.pallas_call(
        functools.partial(reduce_kernel, nx, ny),
        out_shape=jax.ShapeDtypeStruct((tall.shape[1], spread.shape[0]), jnp.float32),
        in_specs=[VMEM, VMEM],
        out_specs=VMEM,
        scratch_shapes=[
            pltpu.VMEM(tall.shape, jnp.bfloat16),
            pltpu.SemaphoreType.DMA((devices,)),
            pltpu.SemaphoreType.DMA((devices,)),
        ],
        compiler_params=pltpu.CompilerParams(
            collective_id=1, has_side_effects=True, vmem_limit_bytes=40 * 2**20
        ),
        name="reduce",
    )(tall, np.ascontiguousarray(spread.T))


def local(
    e_field, h_field, material, permittivity, conductivity, src_shift, src_weight, pupil_mask
):
    nx, ny = lax.axis_size("gx"), lax.axis_size("gy")
    devices = nx * ny
    e, h, near = run_fields(e_field, h_field, material, permittivity, conductivity, nx, ny)
    tall, spread = run_image(src_shift, src_weight, near, pupil_mask, devices)
    image = run_reduce(tall, spread, nx, ny)
    return (image, e, h)


def solution(mesh):
    return jax.shard_map(
        local,
        mesh=mesh,
        in_specs=(
            P(None, None, "gx", "gy"),
            P(None, None, "gx", "gy"),
            P(None, "gx", "gy"),
            P(),
            P(),
            P(("gx", "gy"), None),
            P(("gx", "gy")),
            P(),
        ),
        out_specs=(P(("gx", "gy"), None), P(None, None, "gx", "gy"), P(None, None, "gx", "gy")),
        check_vma=False,
    )
```

```python
import functools

import jax
import jax.numpy as jnp
import numpy as np
from jax import lax
from jax.experimental import pallas as pl
from jax.experimental.pallas import tpu as pltpu
from jax.sharding import PartitionSpec as P

STEPS = 4
K = 256
PW = 128
IMG = 512
COURANT = 0.5
MESH = pl.DeviceIdType.MESH
HIGHEST = lax.Precision.HIGHEST
VMEM = pl.BlockSpec(memory_space=pltpu.VMEM)
SMEM = pl.BlockSpec(memory_space=pltpu.SMEM)
HBM = pl.BlockSpec(memory_space=pltpu.HBM)
CHUNK = 8
FIELDS_MIB = 60


def spectrum_tables(rows_all, cols_all, order):
    freqs = np.arange(order) - order // 2
    phase_y = 2.0 * np.pi * np.mod(np.arange(cols_all)[:, None] * freqs[None, :], cols_all) / cols_all
    table_y = np.concatenate((np.cos(phase_y), -np.sin(phase_y)), axis=1)
    phase_x = 2.0 * np.pi * np.mod(freqs[:, None] * np.arange(rows_all)[None, :], rows_all) / rows_all
    table_x = np.concatenate((np.cos(phase_x), np.sin(phase_x)), axis=1) / np.sqrt(rows_all * cols_all)
    return table_y.astype(np.float32), table_x.astype(np.float32)


def image_tables(window, pixels):
    coarse = pixels // 2
    offsets = np.arange(window) - window // 2
    phase = 2.0 * np.pi * np.mod(offsets[:, None] * np.arange(coarse)[None, :], coarse) / coarse
    cosine, sine = np.cos(phase), np.sin(phase)
    second = np.block([[cosine, sine], [-sine, cosine]])
    first = np.block([[cosine.T, -sine.T], [sine.T, cosine.T]]) / window
    gaps = np.arange(pixels)[:, None] - 2 * np.arange(coarse)[None, :]
    spread = np.ones(gaps.shape)
    for order in range(1, coarse // 2):
        spread += 2.0 * np.cos(2.0 * np.pi * np.mod(order * gaps, pixels) / pixels)
    spread += np.cos(np.pi * gaps / 2.0)
    spread = spread / coarse
    return second.astype(jnp.bfloat16), first.astype(jnp.bfloat16), spread.astype(np.float32)


def greet_all(nx, ny, me):
    barrier = pltpu.get_barrier_semaphore()

    def greet(step, carry):
        other = lax.rem(me + step, nx * ny)
        pl.semaphore_signal(
            barrier, inc=1, device_id=(other // ny, lax.rem(other, ny)), device_id_type=MESH
        )
        return carry

    lax.fori_loop(1, nx * ny, greet, 0)
    pl.semaphore_wait(barrier, nx * ny - 1)


def fields_kernel(
    nx, ny, perm, cond, e_in, h_in, mat_in, e, h, near,
    mat, keep, drive, own, edge_x, up_out, low_out, pack_out, up_in, low_in, pack_in, far_row, far_col,
    in_sem, f_send, f_recv, n_send, n_recv,
):
    depth = mat.shape[0]
    rows, cols = mat.shape[1], mat.shape[2]
    gx, gy = lax.axis_index("gx"), lax.axis_index("gy")
    me = gx * ny + gy
    loads = (
        pltpu.make_async_copy(e_in, e, in_sem.at[0]),
        pltpu.make_async_copy(h_in, h, in_sem.at[1]),
        pltpu.make_async_copy(mat_in, mat, in_sem.at[2]),
    )
    for load in loads:
        load.start()
    for landing in (up_in, low_in, pack_in, far_row, far_col):
        landing[...] = jnp.zeros_like(landing)
    greet_all(nx, ny, me)
    zero = jnp.zeros((rows, cols), jnp.float32)
    lane = lax.broadcasted_iota(jnp.int32, (rows, cols), 1)
    lane3 = lax.broadcasted_iota(jnp.int32, (CHUNK, rows, cols), 2)
    row3 = lax.broadcasted_iota(jnp.int32, (CHUNK, rows, cols), 1)
    keeps, drives = [], []
    for m in range(perm.shape[0]):
        loss = cond[m] / (2.0 * perm[m])
        keeps.append((1.0 - loss) / (1.0 + loss))
        drives.append(COURANT / (perm[m] * (1.0 + loss)))

    west, east = gx > 0, gx < nx - 1
    south, north = gy > 0, gy < ny - 1

    def copies(step):
        routes = (
            (east, west, low_out.at[step], low_in.at[step], 1, 0),
            (west, east, up_out.at[step], up_in.at[step], -1, 0),
            (south, north, pack_out.at[step, 0], pack_in.at[step, 0], 0, -1),
            (north, south, pack_out.at[step, pl.ds(1, 3)], pack_in.at[step, pl.ds(1, 3)], 0, 1),
            (
                jnp.logical_and(east, south), jnp.logical_and(west, north),
                low_out.at[step, 0], far_row.at[step], 1, -1,
            ),
            (
                jnp.logical_and(west, north), jnp.logical_and(east, south),
                pack_out.at[step, 3], far_col.at[step], -1, 1,
            ),
        )
        return [
            (
                sends, gets,
                pltpu.make_async_remote_copy(
                    src_ref=src, dst_ref=dst, send_sem=f_send.at[step, kind],
                    recv_sem=f_recv.at[step, kind], device_id=(gx + dx, gy + dy),
                    device_id_type=MESH,
                ),
            )
            for kind, (sends, gets, src, dst, dx, dy) in enumerate(routes)
        ]

    def packed(parts, edge):
        face = zero
        for k, (field, c) in enumerate(parts):
            for z in range(depth):
                spot = k * depth + z
                moved = pltpu.roll(field[c, z], (spot - edge) % cols, 1)
                face = jnp.where(lane == spot, moved, face)
        return face

    def start(step):
        routes = copies(step)

        def go(kind):
            sends, _, copy = routes[kind]

            @pl.when(sends)
            def _():
                copy.start()

        for k, c in enumerate((1, 2)):
            value = e[c, :, 0, :]
            own[k] = value
            up_out[step, k] = value.astype(jnp.bfloat16)
        go(1)
        pack_out[step, 0] = packed(((e, 0), (e, 2)), 0)
        go(2)
        for k, (field, c) in enumerate(((e, 0), (e, 1), (e, 2), (h, 1), (h, 2))):
            low_out[step, k] = field[c, :, rows - 1, :].astype(jnp.bfloat16)
        go(0)
        go(4)
        pack_out[step, 3] = packed(((e, 1),), cols - 1)
        go(5)
        pack_out[step, 1] = packed(((e, 0), (e, 2)), cols - 1)
        pack_out[step, 2] = packed(((h, 0), (h, 2)), cols - 1)
        go(3)

    def arrive(step, kinds):
        routes = copies(step)
        for kind in kinds:
            _, gets, copy = routes[kind]

            @pl.when(gets)
            def _():
                copy.wait_recv()

    def ghosts(step):
        c_x = jnp.where(west, COURANT, 0.0)
        c_y = jnp.where(south, COURANT, 0.0)
        ex, ey, ez, hy, hz = (low_in[step, k].astype(jnp.float32) for k in range(5))
        flat_z = lax.broadcasted_iota(jnp.int32, (depth, cols), 0)
        flat_y = lax.broadcasted_iota(jnp.int32, (depth, cols), 1)
        corner = pltpu.roll(far_row[step].astype(jnp.float32), cols - 1, 1)
        ex_z = jnp.where(flat_z == depth - 1, 0.0, pltpu.roll(ex, depth - 1, 0))
        ex_y = jnp.where(flat_y == cols - 1, corner, pltpu.roll(ex, cols - 1, 1))
        edge_x[0] = hy - c_x * (ex_z - ex - (own[1] - ez))
        edge_x[1] = hz - c_x * (own[0] - ey - (ex_y - ex))
        row = lax.broadcasted_iota(jnp.int32, (rows, cols), 0)
        e_side, h_side, ey_side = pack_in[step, 1], pack_in[step, 2], pack_in[step, 3]
        across = pltpu.roll(pack_out[step, 0] - e_side, depth, 1)
        ey_z = pltpu.roll(ey_side, cols - 1, 1)
        ey_x = jnp.where(
            row == rows - 1, pltpu.roll(far_col[step], rows - 1, 0), pltpu.roll(ey_side, rows - 1, 0)
        )
        turn_x = across - (ey_z - ey_side)
        turn_z = pltpu.roll(ey_x - ey_side, depth, 1) - across
        return h_side - c_y * jnp.where(lane < depth, turn_x, turn_z)

    def column(face, first, shift):
        return jnp.stack([pltpu.roll(face, (shift - first - z) % cols, 1) for z in range(CHUNK)])

    def above(field, c, base):
        end = min(base + 1 + CHUNK, depth)
        value = field[c, base + 1:end]
        if end == depth:
            value = jnp.concatenate((value, zero[None]), axis=0)
        return value

    def below(field, c, base):
        if base:
            return field[c, base - 1:base - 1 + CHUNK]
        return jnp.concatenate((zero[None], field[c, :CHUNK - 1]), axis=0)

    def magnetic(step):
        face = pack_in[step, 0]
        edge_x[...] = up_in[step].astype(jnp.float32)
        last_row, last_lane = row3 == rows - 1, lane3 == cols - 1
        for base in range(0, depth, CHUNK):
            here = pl.ds(base, CHUNK)
            ex, ey, ez = e[0, here], e[1, here], e[2, here]
            ex_z, ey_z = above(e, 0, base), above(e, 1, base)
            ex_f = column(face, base, cols - 1)
            ez_f = column(face, depth + base, cols - 1)
            ey_x = jnp.where(last_row, edge_x[0, here, :][:, None, :], pltpu.roll(ey, rows - 1, 1))
            ez_x = jnp.where(last_row, edge_x[1, here, :][:, None, :], pltpu.roll(ez, rows - 1, 1))
            ex_y = jnp.where(last_lane, ex_f, pltpu.roll(ex, cols - 1, 2))
            ez_y = jnp.where(last_lane, ez_f, pltpu.roll(ez, cols - 1, 2))
            new_x = h[0, here] - COURANT * (ez_y - ez - (ey_z - ey))
            new_y = h[1, here] - COURANT * (ex_z - ex - (ez_x - ez))
            new_z = h[2, here] - COURANT * (ey_x - ey - (ex_y - ex))
            h[0, here] = new_x
            h[1, here] = new_y
            h[2, here] = new_z

    def electric(face):
        first_row, first_lane = row3 == 0, lane3 == 0
        for base in range(0, depth, CHUNK):
            here = pl.ds(base, CHUNK)
            hx, hy, hz = h[0, here], h[1, here], h[2, here]
            hx_z, hy_z = below(h, 0, base), below(h, 1, base)
            hx_f = column(face, base, 0)
            hz_f = column(face, depth + base, 0)
            hy_x = jnp.where(first_row, edge_x[0, here, :][:, None, :], pltpu.roll(hy, 1, 1))
            hz_x = jnp.where(first_row, edge_x[1, here, :][:, None, :], pltpu.roll(hz, 1, 1))
            hx_y = jnp.where(first_lane, hx_f, pltpu.roll(hx, 1, 2))
            hz_y = jnp.where(first_lane, hz_f, pltpu.roll(hz, 1, 2))
            kept, driven = keep[here], drive[here]
            new_x = kept * e[0, here] + driven * (hz - hz_y - (hy - hy_z))
            new_y = kept * e[1, here] + driven * (hx - hx_z - (hz - hz_x))
            new_z = kept * e[2, here] + driven * (hy - hy_x - (hx - hx_y))
            e[0, here] = new_x
            e[1, here] = new_y
            e[2, here] = new_z

    loads[2].wait()

    for base in range(0, depth, CHUNK):
        index = mat[base:base + CHUNK]
        kept, driven = jnp.zeros_like(index, jnp.float32), jnp.zeros_like(index, jnp.float32)
        for m in range(len(keeps)):
            chosen = index == m
            kept = jnp.where(chosen, keeps[m], kept)
            driven = jnp.where(chosen, drives[m], driven)
        keep[base:base + CHUNK] = kept
        drive[base:base + CHUNK] = driven

    loads[1].wait()
    loads[0].wait()
    start(0)
    for step in range(STEPS):
        if step:
            start(step)
        arrive(step, (1, 2))
        magnetic(step)
        arrive(step, (0, 3, 4, 5))
        electric(ghosts(step))

    def spot(index):
        x_at = pl.multiple_of((index // ny) * rows, rows)
        y_at = pl.multiple_of(lax.rem(index, ny) * cols, cols)
        return near.at[:, pl.ds(x_at, rows), pl.ds(y_at, cols)]

    def near_copy(step, other, place):
        return pltpu.make_async_remote_copy(
            src_ref=e.at[pl.ds(0, 2), depth - 1], dst_ref=spot(place), send_sem=n_send.at[step],
            recv_sem=n_recv.at[step], device_id=(other // ny, lax.rem(other, ny)), device_id_type=MESH,
        )

    def push(step, carry):
        near_copy(step, lax.rem(me + step, nx * ny), me).start()
        return carry

    lax.fori_loop(1, nx * ny, push, 0)
    kept_near = pltpu.make_async_copy(e.at[pl.ds(0, 2), depth - 1], spot(me), n_send.at[0])
    kept_near.start()
    kept_near.wait()

    def take(step, carry):
        copy = near_copy(
            step, lax.rem(me + step, nx * ny), lax.rem(me - step + nx * ny, nx * ny)
        )
        copy.wait_recv()
        copy.wait_send()
        return carry

    lax.fori_loop(1, nx * ny, take, 0)
    for step in range(STEPS):
        for sends, _, copy in copies(step):
            @pl.when(sends)
            def _():
                copy.wait_send()


def run_fields(e_field, h_field, material, permittivity, conductivity, nx, ny):
    _, depth, rows, cols = e_field.shape
    devices = nx * ny
    f32, dma = jnp.float32, pltpu.SemaphoreType.DMA
    return pl.pallas_call(
        functools.partial(fields_kernel, nx, ny),
        out_shape=(
            jax.ShapeDtypeStruct(e_field.shape, f32),
            jax.ShapeDtypeStruct(h_field.shape, f32),
            jax.ShapeDtypeStruct((2, rows * nx, cols * ny), f32),
        ),
        in_specs=[SMEM, SMEM, HBM, HBM, HBM],
        out_specs=(VMEM, VMEM, VMEM),
        scratch_shapes=[
            pltpu.VMEM((depth, rows, cols), jnp.int32),
            pltpu.VMEM((depth, rows, cols), f32),
            pltpu.VMEM((depth, rows, cols), f32),
            pltpu.VMEM((2, depth, cols), f32),
            pltpu.VMEM((2, depth, cols), f32),
            pltpu.VMEM((STEPS, 2, depth, cols), jnp.bfloat16),
            pltpu.VMEM((STEPS, 5, depth, cols), jnp.bfloat16),
            pltpu.VMEM((STEPS, 4, rows, cols), f32),
            pltpu.VMEM((STEPS, 2, depth, cols), jnp.bfloat16),
            pltpu.VMEM((STEPS, 5, depth, cols), jnp.bfloat16),
            pltpu.VMEM((STEPS, 4, rows, cols), f32),
            pltpu.VMEM((STEPS, depth, cols), jnp.bfloat16),
            pltpu.VMEM((STEPS, rows, cols), f32),
            dma((3,)), dma((STEPS, 6)), dma((STEPS, 6)),
            dma((devices,)), dma((devices,)),
        ],
        compiler_params=pltpu.CompilerParams(
            collective_id=0, has_side_effects=True, vmem_limit_bytes=FIELDS_MIB * 2**20
        ),
        name="fields",
    )(permittivity, conductivity, e_field, h_field, material)


def image_kernel(
    sources, shift, weight, near, table_y, table_x, mask, second, first, spread, tall, spec, total,
):
    pols, order = near.shape[0], table_x.shape[0]
    window, coarse = mask.shape[0], spread.shape[1]
    for p in range(pols):
        half = jnp.dot(near[p], table_y[...], precision=HIGHEST, preferred_element_type=jnp.float32)
        real, imag = half[:, :order], half[:, order:]
        both = jnp.concatenate(
            (jnp.concatenate((real, imag), axis=1), jnp.concatenate((imag, -real), axis=1)), axis=0
        )
        value = jnp.dot(table_x[...], both, precision=HIGHEST, preferred_element_type=jnp.float32)
        value = value.astype(jnp.bfloat16).astype(jnp.float32)
        for t in range(spec.shape[1]):
            spec[p, t] = value[:, t * window:(t + 1) * window]
    total[...] = jnp.zeros_like(total)
    keep = mask[...].astype(jnp.float32)

    def add(s, carry):
        a, b = shift[s, 0], shift[s, 1]
        turn = lax.rem(order - b, order)
        pieces = []
        for p in range(pols):
            parts = []
            for k in range(2):
                strip = jnp.concatenate(
                    [
                        spec[p, t, pl.ds(a, window), :]
                        for t in range(k * order // window, (k + 1) * order // window)
                    ],
                    axis=1,
                )
                parts.append(pltpu.roll(strip, turn, 1)[:, :window] * keep)
            pieces.append(jnp.concatenate(parts, axis=1))
        cut = jnp.concatenate(pieces, axis=0).astype(jnp.bfloat16)
        half = jnp.dot(cut, second[...], preferred_element_type=jnp.float32).astype(jnp.bfloat16)
        sides = []
        for p in range(pols):
            part = half[p * window:(p + 1) * window]
            sides.append(jnp.concatenate((part[:, :coarse], part[:, coarse:]), axis=0))
        field = jnp.dot(
            first[...], jnp.concatenate(sides, axis=1), preferred_element_type=jnp.float32
        )
        power = field * field
        power = power[:coarse] + power[coarse:]
        power = sum(power[:, p * coarse:(p + 1) * coarse] for p in range(pols))
        total[...] += weight[s] * (1.0 / sources) * power
        return carry

    lax.fori_loop(0, shift.shape[0], add, 0)
    tall[...] = jnp.dot(
        spread[...], total[...], precision=HIGHEST, preferred_element_type=jnp.float32
    ).astype(jnp.bfloat16).reshape(tall.shape)


def run_image(src_shift, src_weight, near, pupil_mask, devices):
    rows_all, cols_all = near.shape[1], near.shape[2]
    table_y, table_x = spectrum_tables(rows_all, cols_all, K)
    second, first, spread = image_tables(PW, IMG)
    tall = pl.pallas_call(
        functools.partial(image_kernel, src_shift.shape[0] * devices),
        out_shape=jax.ShapeDtypeStruct((IMG, IMG // 2), jnp.bfloat16),
        in_specs=[SMEM, SMEM] + [VMEM] * 7,
        out_specs=VMEM,
        scratch_shapes=[
            pltpu.VMEM((2, 2 * K // PW, K, PW), jnp.float32),
            pltpu.VMEM((IMG // 2, IMG // 2), jnp.float32),
        ],
        compiler_params=pltpu.CompilerParams(vmem_limit_bytes=40 * 2**20),
        name="sources",
    )(src_shift, src_weight, near, table_y, table_x, pupil_mask, second, first, spread)
    return tall.reshape(devices, IMG // devices, IMG // 2), spread


def reduce_kernel(nx, ny, tall, spread, image, got, send, recv):
    devices = nx * ny
    me = lax.axis_index("gx") * ny + lax.axis_index("gy")
    greet_all(nx, ny, me)

    def copy(step, other):
        return pltpu.make_async_remote_copy(
            src_ref=tall.at[other], dst_ref=got.at[step], send_sem=send.at[step],
            recv_sem=recv.at[step], device_id=(other // ny, lax.rem(other, ny)), device_id_type=MESH,
        )

    def push(step, carry):
        copy(step, lax.rem(me + step, devices)).start()
        return carry

    lax.fori_loop(1, devices, push, 0)

    def take(step, total):
        arrived = copy(step, lax.rem(me + step, devices))
        arrived.wait_recv()
        arrived.wait_send()
        return total + got[step].astype(jnp.float32)

    owned = lax.fori_loop(1, devices, take, tall[me].astype(jnp.float32))
    image[...] = jnp.dot(owned, spread[...], precision=HIGHEST, preferred_element_type=jnp.float32)


def run_reduce(tall, spread, nx, ny):
    devices = nx * ny
    return pl.pallas_call(
        functools.partial(reduce_kernel, nx, ny),
        out_shape=jax.ShapeDtypeStruct((tall.shape[1], spread.shape[0]), jnp.float32),
        in_specs=[VMEM, VMEM],
        out_specs=VMEM,
        scratch_shapes=[
            pltpu.VMEM(tall.shape, jnp.bfloat16),
            pltpu.SemaphoreType.DMA((devices,)),
            pltpu.SemaphoreType.DMA((devices,)),
        ],
        compiler_params=pltpu.CompilerParams(
            collective_id=1, has_side_effects=True, vmem_limit_bytes=40 * 2**20
        ),
        name="reduce",
    )(tall, np.ascontiguousarray(spread.T))


def local(
    e_field, h_field, material, permittivity, conductivity, src_shift, src_weight, pupil_mask
):
    nx, ny = lax.axis_size("gx"), lax.axis_size("gy")
    devices = nx * ny
    e, h, near = run_fields(e_field, h_field, material, permittivity, conductivity, nx, ny)
    tall, spread = run_image(src_shift, src_weight, near, pupil_mask, devices)
    image = run_reduce(tall, spread, nx, ny)
    return (image, e, h)


def solution(mesh):
    return jax.shard_map(
        local,
        mesh=mesh,
        in_specs=(
            P(None, None, "gx", "gy"),
            P(None, None, "gx", "gy"),
            P(None, "gx", "gy"),
            P(),
            P(),
            P(("gx", "gy"), None),
            P(("gx", "gy")),
            P(),
        ),
        out_specs=(P(("gx", "gy"), None), P(None, None, "gx", "gy"), P(None, None, "gx", "gy")),
        check_vma=False,
    )
```

```python
import functools

import jax
import jax.numpy as jnp
import numpy as np
from jax import lax
from jax.experimental import pallas as pl
from jax.experimental.pallas import tpu as pltpu
from jax.sharding import PartitionSpec as P

STEPS = 4
K = 256
PW = 128
IMG = 512
COURANT = 0.5
MESH = pl.DeviceIdType.MESH
HIGHEST = lax.Precision.HIGHEST
VMEM = pl.BlockSpec(memory_space=pltpu.VMEM)
SMEM = pl.BlockSpec(memory_space=pltpu.SMEM)
HBM = pl.BlockSpec(memory_space=pltpu.HBM)
CHUNK = 8
FIELDS_MIB = 60


def spectrum_tables(rows_all, cols_all, order):
    freqs = np.arange(order) - order // 2
    phase_y = 2.0 * np.pi * np.mod(np.arange(cols_all)[:, None] * freqs[None, :], cols_all) / cols_all
    table_y = np.concatenate((np.cos(phase_y), -np.sin(phase_y)), axis=1)
    phase_x = 2.0 * np.pi * np.mod(freqs[:, None] * np.arange(rows_all)[None, :], rows_all) / rows_all
    table_x = np.concatenate((np.cos(phase_x), np.sin(phase_x)), axis=1) / np.sqrt(rows_all * cols_all)
    return table_y.astype(np.float32), table_x.astype(np.float32)


def image_tables(window, pixels):
    coarse = pixels // 2
    offsets = np.arange(window) - window // 2
    phase = 2.0 * np.pi * np.mod(offsets[:, None] * np.arange(coarse)[None, :], coarse) / coarse
    cosine, sine = np.cos(phase), np.sin(phase)
    second = np.block([[cosine, sine], [-sine, cosine]])
    first = np.block([[cosine.T, -sine.T], [sine.T, cosine.T]]) / window
    gaps = np.arange(pixels)[:, None] - 2 * np.arange(coarse)[None, :]
    spread = np.ones(gaps.shape)
    for order in range(1, coarse // 2):
        spread += 2.0 * np.cos(2.0 * np.pi * np.mod(order * gaps, pixels) / pixels)
    spread += np.cos(np.pi * gaps / 2.0)
    spread = spread / coarse
    return second.astype(jnp.bfloat16), first.astype(jnp.bfloat16), spread.astype(np.float32)


def greet_all(nx, ny, me):
    barrier = pltpu.get_barrier_semaphore()

    def greet(step, carry):
        other = lax.rem(me + step, nx * ny)
        pl.semaphore_signal(
            barrier, inc=1, device_id=(other // ny, lax.rem(other, ny)), device_id_type=MESH
        )
        return carry

    lax.fori_loop(1, nx * ny, greet, 0)
    pl.semaphore_wait(barrier, nx * ny - 1)


def fields_kernel(
    nx, ny, perm, cond, e_in, h_in, mat_in, e, h, near,
    mat, keep, drive, own, edge_x, up_out, low_out, pack_out, up_in, low_in, pack_in, far_row, far_col,
    in_sem, f_send, f_recv, n_send, n_recv,
):
    depth = mat.shape[0]
    rows, cols = mat.shape[1], mat.shape[2]
    gx, gy = lax.axis_index("gx"), lax.axis_index("gy")
    me = gx * ny + gy
    loads = (
        pltpu.make_async_copy(e_in, e, in_sem.at[0]),
        pltpu.make_async_copy(h_in, h, in_sem.at[1]),
        pltpu.make_async_copy(mat_in, mat, in_sem.at[2]),
    )
    for load in loads:
        load.start()
    for landing in (up_in, low_in, pack_in, far_row, far_col):
        landing[...] = jnp.zeros_like(landing)
    greet_all(nx, ny, me)
    zero = jnp.zeros((rows, cols), jnp.float32)
    lane = lax.broadcasted_iota(jnp.int32, (rows, cols), 1)
    lane3 = lax.broadcasted_iota(jnp.int32, (CHUNK, rows, cols), 2)
    row3 = lax.broadcasted_iota(jnp.int32, (CHUNK, rows, cols), 1)
    keeps, drives = [], []
    for m in range(perm.shape[0]):
        loss = cond[m] / (2.0 * perm[m])
        keeps.append((1.0 - loss) / (1.0 + loss))
        drives.append(COURANT / (perm[m] * (1.0 + loss)))

    west, east = gx > 0, gx < nx - 1
    south, north = gy > 0, gy < ny - 1

    def copies(step):
        routes = (
            (east, west, low_out.at[step], low_in.at[step], 1, 0),
            (west, east, up_out.at[step], up_in.at[step], -1, 0),
            (south, north, pack_out.at[step, 0], pack_in.at[step, 0], 0, -1),
            (north, south, pack_out.at[step, pl.ds(1, 3)], pack_in.at[step, pl.ds(1, 3)], 0, 1),
            (
                jnp.logical_and(east, south), jnp.logical_and(west, north),
                low_out.at[step, 0], far_row.at[step], 1, -1,
            ),
            (
                jnp.logical_and(west, north), jnp.logical_and(east, south),
                pack_out.at[step, 3], far_col.at[step], -1, 1,
            ),
        )
        return [
            (
                sends, gets,
                pltpu.make_async_remote_copy(
                    src_ref=src, dst_ref=dst, send_sem=f_send.at[step, kind],
                    recv_sem=f_recv.at[step, kind], device_id=(gx + dx, gy + dy),
                    device_id_type=MESH,
                ),
            )
            for kind, (sends, gets, src, dst, dx, dy) in enumerate(routes)
        ]

    def packed(parts, edge):
        face = zero
        for k, (field, c) in enumerate(parts):
            for z in range(depth):
                spot = k * depth + z
                moved = pltpu.roll(field[c, z], (spot - edge) % cols, 1)
                face = jnp.where(lane == spot, moved, face)
        return face

    def both_sides(parts):
        low, high = zero, zero
        for k, (field, c) in enumerate(parts):
            for z in range(depth):
                spot = k * depth + z
                moved = pltpu.roll(field[c, z], spot, 1) if spot else field[c, z]
                low = jnp.where(lane == spot, moved, low)
                high = jnp.where(lane == (spot - 1) % cols, moved, high)
        return low, pltpu.roll(high, 1, 1)

    def start(step):
        routes = copies(step)

        def go(kind):
            sends, _, copy = routes[kind]

            @pl.when(sends)
            def _():
                copy.start()

        for k, c in enumerate((1, 2)):
            value = e[c, :, 0, :]
            own[k] = value
            up_out[step, k] = value.astype(jnp.bfloat16)
        go(1)
        pack_out[step, 0], pack_out[step, 1] = both_sides(((e, 0), (e, 2)))
        go(2)
        for k, (field, c) in enumerate(((e, 0), (e, 1), (e, 2), (h, 1), (h, 2))):
            low_out[step, k] = field[c, :, rows - 1, :].astype(jnp.bfloat16)
        go(0)
        go(4)
        pack_out[step, 3] = packed(((e, 1),), cols - 1)
        go(5)
        pack_out[step, 2] = packed(((h, 0), (h, 2)), cols - 1)
        go(3)

    def arrive(step, kinds):
        routes = copies(step)
        for kind in kinds:
            _, gets, copy = routes[kind]

            @pl.when(gets)
            def _():
                copy.wait_recv()

    def ghosts(step):
        c_x = jnp.where(west, COURANT, 0.0)
        c_y = jnp.where(south, COURANT, 0.0)
        ex, ey, ez, hy, hz = (low_in[step, k].astype(jnp.float32) for k in range(5))
        flat_z = lax.broadcasted_iota(jnp.int32, (depth, cols), 0)
        flat_y = lax.broadcasted_iota(jnp.int32, (depth, cols), 1)
        corner = pltpu.roll(far_row[step].astype(jnp.float32), cols - 1, 1)
        ex_z = jnp.where(flat_z == depth - 1, 0.0, pltpu.roll(ex, depth - 1, 0))
        ex_y = jnp.where(flat_y == cols - 1, corner, pltpu.roll(ex, cols - 1, 1))
        edge_x[0] = hy - c_x * (ex_z - ex - (own[1] - ez))
        edge_x[1] = hz - c_x * (own[0] - ey - (ex_y - ex))
        row = lax.broadcasted_iota(jnp.int32, (rows, cols), 0)
        e_side, h_side, ey_side = pack_in[step, 1], pack_in[step, 2], pack_in[step, 3]
        across = pltpu.roll(pack_out[step, 0] - e_side, depth, 1)
        ey_z = pltpu.roll(ey_side, cols - 1, 1)
        ey_x = jnp.where(
            row == rows - 1, pltpu.roll(far_col[step], rows - 1, 0), pltpu.roll(ey_side, rows - 1, 0)
        )
        turn_x = across - (ey_z - ey_side)
        turn_z = pltpu.roll(ey_x - ey_side, depth, 1) - across
        return h_side - c_y * jnp.where(lane < depth, turn_x, turn_z)

    def column(face, first, shift):
        return jnp.stack([pltpu.roll(face, (shift - first - z) % cols, 1) for z in range(CHUNK)])

    def above(field, c, base):
        end = min(base + 1 + CHUNK, depth)
        value = field[c, base + 1:end]
        if end == depth:
            value = jnp.concatenate((value, zero[None]), axis=0)
        return value

    def below(field, c, base):
        if base:
            return field[c, base - 1:base - 1 + CHUNK]
        return jnp.concatenate((zero[None], field[c, :CHUNK - 1]), axis=0)

    def magnetic(step):
        face = pack_in[step, 0]
        edge_x[...] = up_in[step].astype(jnp.float32)
        last_row, last_lane = row3 == rows - 1, lane3 == cols - 1
        for base in range(0, depth, CHUNK):
            here = pl.ds(base, CHUNK)
            ex, ey, ez = e[0, here], e[1, here], e[2, here]
            ex_z, ey_z = above(e, 0, base), above(e, 1, base)
            ex_f = column(face, base, cols - 1)
            ez_f = column(face, depth + base, cols - 1)
            ey_x = jnp.where(last_row, edge_x[0, here, :][:, None, :], pltpu.roll(ey, rows - 1, 1))
            ez_x = jnp.where(last_row, edge_x[1, here, :][:, None, :], pltpu.roll(ez, rows - 1, 1))
            ex_y = jnp.where(last_lane, ex_f, pltpu.roll(ex, cols - 1, 2))
            ez_y = jnp.where(last_lane, ez_f, pltpu.roll(ez, cols - 1, 2))
            new_x = h[0, here] - COURANT * (ez_y - ez - (ey_z - ey))
            new_y = h[1, here] - COURANT * (ex_z - ex - (ez_x - ez))
            new_z = h[2, here] - COURANT * (ey_x - ey - (ex_y - ex))
            h[0, here] = new_x
            h[1, here] = new_y
            h[2, here] = new_z

    def electric(face):
        first_row, first_lane = row3 == 0, lane3 == 0
        for base in range(0, depth, CHUNK):
            here = pl.ds(base, CHUNK)
            hx, hy, hz = h[0, here], h[1, here], h[2, here]
            hx_z, hy_z = below(h, 0, base), below(h, 1, base)
            hx_f = column(face, base, 0)
            hz_f = column(face, depth + base, 0)
            hy_x = jnp.where(first_row, edge_x[0, here, :][:, None, :], pltpu.roll(hy, 1, 1))
            hz_x = jnp.where(first_row, edge_x[1, here, :][:, None, :], pltpu.roll(hz, 1, 1))
            hx_y = jnp.where(first_lane, hx_f, pltpu.roll(hx, 1, 2))
            hz_y = jnp.where(first_lane, hz_f, pltpu.roll(hz, 1, 2))
            kept, driven = keep[here], drive[here]
            new_x = kept * e[0, here] + driven * (hz - hz_y - (hy - hy_z))
            new_y = kept * e[1, here] + driven * (hx - hx_z - (hz - hz_x))
            new_z = kept * e[2, here] + driven * (hy - hy_x - (hx - hx_y))
            e[0, here] = new_x
            e[1, here] = new_y
            e[2, here] = new_z

    loads[2].wait()

    for base in range(0, depth, CHUNK):
        index = mat[base:base + CHUNK]
        kept, driven = jnp.zeros_like(index, jnp.float32), jnp.zeros_like(index, jnp.float32)
        for m in range(len(keeps)):
            chosen = index == m
            kept = jnp.where(chosen, keeps[m], kept)
            driven = jnp.where(chosen, drives[m], driven)
        keep[base:base + CHUNK] = kept
        drive[base:base + CHUNK] = driven

    loads[1].wait()
    loads[0].wait()
    start(0)
    for step in range(STEPS):
        if step:
            start(step)
        arrive(step, (1, 2))
        magnetic(step)
        arrive(step, (0, 3, 4, 5))
        electric(ghosts(step))

    def spot(index):
        x_at = pl.multiple_of((index // ny) * rows, rows)
        y_at = pl.multiple_of(lax.rem(index, ny) * cols, cols)
        return near.at[:, pl.ds(x_at, rows), pl.ds(y_at, cols)]

    def near_copy(step, other, place):
        return pltpu.make_async_remote_copy(
            src_ref=e.at[pl.ds(0, 2), depth - 1], dst_ref=spot(place), send_sem=n_send.at[step],
            recv_sem=n_recv.at[step], device_id=(other // ny, lax.rem(other, ny)), device_id_type=MESH,
        )

    def push(step, carry):
        near_copy(step, lax.rem(me + step, nx * ny), me).start()
        return carry

    lax.fori_loop(1, nx * ny, push, 0)
    kept_near = pltpu.make_async_copy(e.at[pl.ds(0, 2), depth - 1], spot(me), n_send.at[0])
    kept_near.start()
    kept_near.wait()

    def take(step, carry):
        copy = near_copy(
            step, lax.rem(me + step, nx * ny), lax.rem(me - step + nx * ny, nx * ny)
        )
        copy.wait_recv()
        copy.wait_send()
        return carry

    lax.fori_loop(1, nx * ny, take, 0)
    for step in range(STEPS):
        for sends, _, copy in copies(step):
            @pl.when(sends)
            def _():
                copy.wait_send()


def run_fields(e_field, h_field, material, permittivity, conductivity, nx, ny):
    _, depth, rows, cols = e_field.shape
    devices = nx * ny
    f32, dma = jnp.float32, pltpu.SemaphoreType.DMA
    return pl.pallas_call(
        functools.partial(fields_kernel, nx, ny),
        out_shape=(
            jax.ShapeDtypeStruct(e_field.shape, f32),
            jax.ShapeDtypeStruct(h_field.shape, f32),
            jax.ShapeDtypeStruct((2, rows * nx, cols * ny), f32),
        ),
        in_specs=[SMEM, SMEM, HBM, HBM, HBM],
        out_specs=(VMEM, VMEM, VMEM),
        scratch_shapes=[
            pltpu.VMEM((depth, rows, cols), jnp.int32),
            pltpu.VMEM((depth, rows, cols), f32),
            pltpu.VMEM((depth, rows, cols), f32),
            pltpu.VMEM((2, depth, cols), f32),
            pltpu.VMEM((2, depth, cols), f32),
            pltpu.VMEM((STEPS, 2, depth, cols), jnp.bfloat16),
            pltpu.VMEM((STEPS, 5, depth, cols), jnp.bfloat16),
            pltpu.VMEM((STEPS, 4, rows, cols), f32),
            pltpu.VMEM((STEPS, 2, depth, cols), jnp.bfloat16),
            pltpu.VMEM((STEPS, 5, depth, cols), jnp.bfloat16),
            pltpu.VMEM((STEPS, 4, rows, cols), f32),
            pltpu.VMEM((STEPS, depth, cols), jnp.bfloat16),
            pltpu.VMEM((STEPS, rows, cols), f32),
            dma((3,)), dma((STEPS, 6)), dma((STEPS, 6)),
            dma((devices,)), dma((devices,)),
        ],
        compiler_params=pltpu.CompilerParams(
            collective_id=0, has_side_effects=True, vmem_limit_bytes=FIELDS_MIB * 2**20
        ),
        name="fields",
    )(permittivity, conductivity, e_field, h_field, material)


def image_kernel(
    sources, shift, weight, near, table_y, table_x, mask, second, first, spread, tall, spec, total,
):
    pols, order = near.shape[0], table_x.shape[0]
    window, coarse = mask.shape[0], spread.shape[1]
    for p in range(pols):
        half = jnp.dot(near[p], table_y[...], precision=HIGHEST, preferred_element_type=jnp.float32)
        real, imag = half[:, :order], half[:, order:]
        both = jnp.concatenate(
            (jnp.concatenate((real, imag), axis=1), jnp.concatenate((imag, -real), axis=1)), axis=0
        )
        value = jnp.dot(table_x[...], both, precision=HIGHEST, preferred_element_type=jnp.float32)
        value = value.astype(jnp.bfloat16).astype(jnp.float32)
        for t in range(spec.shape[1]):
            spec[p, t] = value[:, t * window:(t + 1) * window]
    total[...] = jnp.zeros_like(total)
    keep = mask[...].astype(jnp.float32)

    def add(s, carry):
        a, b = shift[s, 0], shift[s, 1]
        turn = lax.rem(order - b, order)
        pieces = []
        for p in range(pols):
            parts = []
            for k in range(2):
                strip = jnp.concatenate(
                    [
                        spec[p, t, pl.ds(a, window), :]
                        for t in range(k * order // window, (k + 1) * order // window)
                    ],
                    axis=1,
                )
                parts.append(pltpu.roll(strip, turn, 1)[:, :window] * keep)
            pieces.append(jnp.concatenate(parts, axis=1))
        cut = jnp.concatenate(pieces, axis=0).astype(jnp.bfloat16)
        half = jnp.dot(cut, second[...], preferred_element_type=jnp.float32).astype(jnp.bfloat16)
        sides = []
        for p in range(pols):
            part = half[p * window:(p + 1) * window]
            sides.append(jnp.concatenate((part[:, :coarse], part[:, coarse:]), axis=0))
        field = jnp.dot(
            first[...], jnp.concatenate(sides, axis=1), preferred_element_type=jnp.float32
        )
        power = field * field
        power = power[:coarse] + power[coarse:]
        power = sum(power[:, p * coarse:(p + 1) * coarse] for p in range(pols))
        total[...] += weight[s] * (1.0 / sources) * power
        return carry

    lax.fori_loop(0, shift.shape[0], add, 0)
    tall[...] = jnp.dot(
        spread[...], total[...], precision=HIGHEST, preferred_element_type=jnp.float32
    ).astype(jnp.bfloat16).reshape(tall.shape)


def run_image(src_shift, src_weight, near, pupil_mask, devices):
    rows_all, cols_all = near.shape[1], near.shape[2]
    table_y, table_x = spectrum_tables(rows_all, cols_all, K)
    second, first, spread = image_tables(PW, IMG)
    tall = pl.pallas_call(
        functools.partial(image_kernel, src_shift.shape[0] * devices),
        out_shape=jax.ShapeDtypeStruct((IMG, IMG // 2), jnp.bfloat16),
        in_specs=[SMEM, SMEM] + [VMEM] * 7,
        out_specs=VMEM,
        scratch_shapes=[
            pltpu.VMEM((2, 2 * K // PW, K, PW), jnp.float32),
            pltpu.VMEM((IMG // 2, IMG // 2), jnp.float32),
        ],
        compiler_params=pltpu.CompilerParams(vmem_limit_bytes=40 * 2**20),
        name="sources",
    )(src_shift, src_weight, near, table_y, table_x, pupil_mask, second, first, spread)
    return tall.reshape(devices, IMG // devices, IMG // 2), spread


def reduce_kernel(nx, ny, tall, spread, image, got, send, recv):
    devices = nx * ny
    me = lax.axis_index("gx") * ny + lax.axis_index("gy")
    greet_all(nx, ny, me)

    def copy(step, other):
        return pltpu.make_async_remote_copy(
            src_ref=tall.at[other], dst_ref=got.at[step], send_sem=send.at[step],
            recv_sem=recv.at[step], device_id=(other // ny, lax.rem(other, ny)), device_id_type=MESH,
        )

    def push(step, carry):
        copy(step, lax.rem(me + step, devices)).start()
        return carry

    lax.fori_loop(1, devices, push, 0)

    def take(step, total):
        arrived = copy(step, lax.rem(me + step, devices))
        arrived.wait_recv()
        arrived.wait_send()
        return total + got[step].astype(jnp.float32)

    owned = lax.fori_loop(1, devices, take, tall[me].astype(jnp.float32))
    image[...] = jnp.dot(owned, spread[...], precision=HIGHEST, preferred_element_type=jnp.float32)


def run_reduce(tall, spread, nx, ny):
    devices = nx * ny
    return pl.pallas_call(
        functools.partial(reduce_kernel, nx, ny),
        out_shape=jax.ShapeDtypeStruct((tall.shape[1], spread.shape[0]), jnp.float32),
        in_specs=[VMEM, VMEM],
        out_specs=VMEM,
        scratch_shapes=[
            pltpu.VMEM(tall.shape, jnp.bfloat16),
            pltpu.SemaphoreType.DMA((devices,)),
            pltpu.SemaphoreType.DMA((devices,)),
        ],
        compiler_params=pltpu.CompilerParams(
            collective_id=1, has_side_effects=True, vmem_limit_bytes=40 * 2**20
        ),
        name="reduce",
    )(tall, np.ascontiguousarray(spread.T))


def local(
    e_field, h_field, material, permittivity, conductivity, src_shift, src_weight, pupil_mask
):
    nx, ny = lax.axis_size("gx"), lax.axis_size("gy")
    devices = nx * ny
    e, h, near = run_fields(e_field, h_field, material, permittivity, conductivity, nx, ny)
    tall, spread = run_image(src_shift, src_weight, near, pupil_mask, devices)
    image = run_reduce(tall, spread, nx, ny)
    return (image, e, h)


def solution(mesh):
    return jax.shard_map(
        local,
        mesh=mesh,
        in_specs=(
            P(None, None, "gx", "gy"),
            P(None, None, "gx", "gy"),
            P(None, "gx", "gy"),
            P(),
            P(),
            P(("gx", "gy"), None),
            P(("gx", "gy")),
            P(),
        ),
        out_specs=(P(("gx", "gy"), None), P(None, None, "gx", "gy"), P(None, None, "gx", "gy")),
        check_vma=False,
    )
```
